32 devices in a mesh: group: 2 (over x), pos: 16 (over z, y, core).
Axes of the slice: x: 2, y: 2, z: 4, core: 2. Of those that a mesh axis runs over, the one named last changes fastest.
Arguments:
- acts: bfloat16 [4, 1024, 1536], P('group', 'pos'), parts along dimension 0, may hold values from -12 to 12
- skips: bfloat16 [4, 2048, 1280], P('group', 'pos'), parts along dimension 0, may hold values from -6 to 6
- norm_gain: float32 [1536], replicated, may hold values from 0.6 to 1.6
- w_query: bfloat16 [1536, 256], replicated, may hold values from -4 to 4
- w_key: bfloat16 [1536, 256], replicated, may hold values from -4 to 4
- w_value: bfloat16 [1536, 768], replicated, may hold values from -0.15625 to 0.15625
- w_out: bfloat16 [768, 1536], replicated, may hold values from -0.21875 to 0.21875
- w_lift: bfloat16 [1536, 1536], P('pos'), may hold values from -0.15625 to 0.15625
- w_skip: bfloat16 [1280, 1536], P('pos'), may hold values from -0.15625 to 0.15625
- depth_kernel: float32 [3, 1536], replicated, may hold values from -3 to 3
- w_point: bfloat16 [1536, 1536], P(None, 'pos'), may hold values from -0.15625 to 0.15625
Outputs:
- decoded: bfloat16 [4, 2048, 1536], P('group', 'pos'), parts along dimension 0
The draws below stay inside these ranges and needn't reach their ends.
There are 2 independent parts, one for each index of `group`. The reference program is written for one: setup_inputs(seed, part) draws one part's arguments, and reference() takes and returns one part's arrays. A program takes and returns all parts, laid end to end along the dimension named above; an argument that names none is the same for every part. Nothing has to cross between parts.
All inputs are finite; a program needn't handle non-finite values.
Results may differ from the reference program's by a relative error of at most 0.014.
Values may be sent and summed in bfloat16 or wider, within the bound.
No kernel may reach another device: no remote copies, remote signals or barrier semaphores. Data moves between devices by JAX's collectives and lax.ppermute only.
A program may use at most 128 MiB of HBM per device.

```python
import jax
import jax.numpy as jnp
from jax import lax

D = 1536
CS = 1280
HEADS = 4
HK = 64
HV = 192
SEQS = 2
BINS = 1024


def marked_layout(feature_count, head_count):
    per_head = 8
    spacing = feature_count // (per_head * head_count)
    slot_ids = jnp.arange(per_head * head_count, dtype=jnp.int32)
    owner_head = slot_ids % head_count
    sign_values = jnp.where(slot_ids // head_count % 2 == 0, 1.0, -1.0).astype(jnp.float32)
    pattern = jnp.zeros((head_count, feature_count), jnp.float32)
    return pattern.at[owner_head, slot_ids * spacing].set(sign_values / jnp.sqrt(jnp.float32(per_head)))


def unit_rows(raw_noise, support):
    free_count = raw_noise.shape[-1] - jnp.sum(support.astype(jnp.float32))
    raw_noise = jnp.where(support, 0.0, raw_noise)
    raw_noise = raw_noise - jnp.sum(raw_noise, axis=-1, keepdims=True) / free_count
    raw_noise = jnp.where(support, 0.0, raw_noise)
    return raw_noise * jnp.sqrt(raw_noise.shape[-1] / jnp.sum(raw_noise * raw_noise, axis=-1, keepdims=True))


def draw_acts(key, part):
    pattern = marked_layout(D, HEADS)
    support = jnp.sum(jnp.abs(pattern), axis=0) > 0.0
    direction = jnp.sum(pattern, axis=0) / jnp.sqrt(jnp.float32(HEADS))
    noise_key, place_key, level_key = jax.random.split(key, 3)
    raw_noise = jnp.clip(jax.random.normal(noise_key, (SEQS, BINS, D), jnp.float32), -4.0, 4.0)
    unit_noise = unit_rows(raw_noise, support)
    starts = jax.random.randint(place_key, (SEQS,), 0, BINS - 5).astype(jnp.int32)
    places = (starts[:, None] + jnp.arange(6, dtype=jnp.int32)[None, :]).astype(jnp.int32)
    tier_levels = 0.955 + 0.01 * jnp.arange(3, dtype=jnp.float32)
    upper_level = tier_levels[None, :] + jax.random.uniform(level_key, (SEQS, 3), jnp.float32, 0.0, 0.006)
    levels = jnp.stack([upper_level, upper_level - 0.0085], axis=-1).reshape(SEQS, 6)
    chosen = jnp.take_along_axis(unit_noise, places[:, :, None], axis=1)
    marked = levels[..., None] * jnp.sqrt(jnp.float32(D)) * direction + jnp.sqrt(1.0 - levels * levels)[..., None] * chosen
    seq_rows = jnp.arange(SEQS, dtype=jnp.int32)[:, None]
    drawn_acts = unit_noise.at[seq_rows, places].set(marked)
    return drawn_acts.astype(jnp.bfloat16)


def draw_norm_gain(key, part):
    pattern = marked_layout(D, HEADS)
    support = jnp.sum(jnp.abs(pattern), axis=0) > 0.0
    wide_key, steady_key = jax.random.split(jax.random.fold_in(key, 3))
    wide_gain = jax.random.uniform(wide_key, (D,), jnp.float32, 0.6, 1.4)
    steady_gain = jax.random.uniform(steady_key, (D,), jnp.float32, 0.97, 1.03)
    return jnp.where(support, steady_gain, wide_gain)


def query_key_weight(key, offset_id):
    pattern = marked_layout(D, HEADS)
    support = jnp.sum(jnp.abs(pattern), axis=0) > 0.0
    angle_key, order_key = jax.random.split(jax.random.fold_in(key, 7))
    heading = jax.random.normal(angle_key, (HEADS, HK), jnp.float32)
    heading = heading / jnp.sqrt(jnp.sum(heading * heading, axis=-1, keepdims=True))
    ranking = jax.random.permutation(order_key, HEADS).astype(jnp.float32)
    strength = 0.5 + 0.5 * ranking / max(HEADS - 1, 1)
    factor = jnp.sqrt(320.0 * HEADS * jnp.sqrt(jnp.float32(HK)) / D)
    column_scale = 1.33 * jnp.exp(jax.random.uniform(jax.random.fold_in(key, 9), (HEADS, HK), jnp.float32, jnp.log(0.5), jnp.log(2.0)))
    random_part = jnp.clip(jax.random.normal(jax.random.fold_in(key, offset_id), (D, HEADS, HK), jnp.float32), -6.0, 6.0) / jnp.sqrt(jnp.float32(D))
    random_part = random_part * column_scale[None]
    random_part = jnp.where(support[:, None, None], 0.0, random_part)
    component = jnp.sum(random_part * heading[None], axis=-1, keepdims=True)
    remaining = random_part - component * heading[None]
    planted = factor * pattern.T[:, :, None] * (jnp.sqrt(strength)[:, None] * heading)[None]
    return (remaining + planted).reshape(D, HEADS * HK)


def draw_w_query(key, part):
    return query_key_weight(key, 21).astype(jnp.bfloat16)


def draw_w_key(key, part):
    return query_key_weight(key, 22).astype(jnp.bfloat16)


def level_of(key, shape, pieces, least, high):
    level, own = 1.0, jax.random.fold_in(key, 6)
    for dim, blocks in pieces:
        draws = jnp.exp(jax.random.uniform(jax.random.fold_in(own, dim), (blocks,), jnp.float32, least / len(pieces), high / len(pieces)))
        level = level * jnp.repeat(draws, shape[dim] // blocks).reshape([-1 if axis == dim else 1 for axis in range(len(shape))])
    return level


def normal_values(rng, dims, scale, reach, pieces=(), held_as=jnp.bfloat16):
    entries = jax.random.normal(rng, dims, jnp.float32) * scale
    if len(pieces) > 0:
        entries = level_of(rng, dims, pieces, -0.22, 0.18) * entries
    return jnp.clip(entries, min=-reach, max=reach).astype(held_as)


def setup_inputs(seed: int = 0, part: int = 0) -> dict:
    keys = jax.random.split(jax.random.key(seed), 12)
    own_keys = jax.random.split(jax.random.fold_in(keys[11], part), 12)
    acts = draw_acts(jax.random.fold_in(jax.random.fold_in(keys[11], part), 71), part)
    skips = normal_values(own_keys[1], (SEQS, 2 * BINS, CS), 1.0, 6.0, ((1, 16),))
    norm_gain = draw_norm_gain(jax.random.fold_in(keys[11], 71), part)
    w_query = draw_w_query(jax.random.fold_in(keys[11], 71), part)
    w_key = draw_w_key(jax.random.fold_in(keys[11], 71), part)
    w_value = normal_values(keys[5], (D, HEADS * HV), D ** -0.5, 0.15625)
    w_out = normal_values(keys[6], (HEADS * HV, D), (HEADS * HV) ** -0.5, 0.21875)
    w_lift = normal_values(keys[7], (D, D), D ** -0.5, 0.15625, ((0, 16),))
    w_skip = normal_values(keys[8], (CS, D), CS ** -0.5, 0.15625, ((0, 16),))
    depth_kernel = normal_values(keys[9], (3, D), 0.6, 3.0, (), jnp.float32)
    w_point = normal_values(keys[10], (D, D), D ** -0.5, 0.15625, ((1, 16),))
    return dict(acts=acts, skips=skips, norm_gain=norm_gain, w_query=w_query, w_key=w_key, w_value=w_value, w_out=w_out, w_lift=w_lift, w_skip=w_skip, depth_kernel=depth_kernel, w_point=w_point)


def reference(acts, skips, norm_gain, w_query, w_key, w_value, w_out, w_lift, w_skip, depth_kernel, w_point):
    actsf = acts.astype(jnp.float32)
    centre = actsf - lax.optimization_barrier(jnp.mean(actsf, axis=-1, keepdims=True))
    normed = (centre * lax.rsqrt(lax.optimization_barrier(jnp.mean(centre * centre, axis=-1, keepdims=True)) + 1e-05) * norm_gain).astype(jnp.bfloat16)
    flat = normed.reshape(SEQS * BINS, D)
    queries = (jnp.dot(flat, w_query, preferred_element_type=jnp.float32) * HK ** (-0.5)).astype(jnp.bfloat16).reshape(SEQS, BINS, HEADS, HK)
    keyed = jnp.dot(flat, w_key, preferred_element_type=jnp.float32).astype(jnp.bfloat16).reshape(SEQS, BINS, HEADS, HK)
    valued = jnp.dot(flat, w_value, preferred_element_type=jnp.float32).astype(jnp.bfloat16).reshape(SEQS, BINS, HEADS, HV)
    block = min(512, BINS)
    nblocks = BINS // block

    def attend(index):
        part = lax.dynamic_slice_in_dim(queries, (index * block).astype(jnp.int32), block, 1)
        scores = jnp.einsum('sqhd,skhd->shqk', part.astype(jnp.float32), keyed.astype(jnp.float32))
        highest = lax.optimization_barrier(jnp.max(scores, axis=-1, keepdims=True))
        weights = jnp.exp(scores - highest)
        totals = lax.optimization_barrier(jnp.sum(weights, axis=-1))
        summed = jnp.einsum('shqk,skhv->shqv', weights.astype(jnp.bfloat16).astype(jnp.float32), valued.astype(jnp.float32))
        return (summed / totals[..., None]).transpose(0, 2, 1, 3)
    blocks = lax.map(attend, jnp.arange(nblocks, dtype=jnp.int32))
    mixed = blocks.transpose(1, 0, 2, 3, 4).reshape(SEQS * BINS, HEADS * HV).astype(jnp.bfloat16)
    attended = (actsf.reshape(SEQS * BINS, D) + jnp.dot(mixed, w_out, preferred_element_type=jnp.float32)).astype(jnp.bfloat16)
    activated = jax.nn.gelu(attended.astype(jnp.float32)).astype(jnp.bfloat16)
    lifted = jnp.dot(activated, w_lift, preferred_element_type=jnp.float32).astype(jnp.bfloat16).reshape(SEQS, BINS, D)
    raised = jnp.repeat(lifted, 2, axis=1).reshape(SEQS * 2 * BINS, D)
    skip_act = jax.nn.gelu(skips.astype(jnp.float32)).astype(jnp.bfloat16).reshape(SEQS * 2 * BINS, CS)
    merged = (raised.astype(jnp.float32) + jnp.dot(skip_act, w_skip, preferred_element_type=jnp.float32)).astype(jnp.bfloat16).reshape(SEQS, 2 * BINS, D)
    padded = jnp.pad(merged.astype(jnp.float32), ((0, 0), (1, 1), (0, 0)))
    spread = (depth_kernel[0] * padded[:, :-2] + depth_kernel[1] * padded[:, 1:-1] + depth_kernel[2] * padded[:, 2:]).astype(jnp.bfloat16)
    decoded = jnp.dot(spread.reshape(SEQS * 2 * BINS, D), w_point, preferred_element_type=jnp.float32)
    return decoded.astype(jnp.bfloat16).reshape(SEQS, 2 * BINS, D)
```

```python
import functools

import jax
import jax.numpy as jnp
from jax import lax
from jax.experimental import pallas as pl
from jax.experimental.pallas import tpu as pltpu
from jax.sharding import PartitionSpec as P

HEADS = 4
HK = 64
HV = 192
F32 = jnp.float32
BF16 = jnp.bfloat16
ANY = pl.BlockSpec(memory_space=pl.ANY)
VMEM = pl.BlockSpec(memory_space=pltpu.VMEM)
SMEM = pl.BlockSpec(memory_space=pltpu.SMEM)
LIMIT = pltpu.CompilerParams(vmem_limit_bytes=40 * 1024 * 1024)

POS = 16
C_SWAP = [(i, i ^ 1) for i in range(POS)]
Y_SWAP = [(i, i ^ 2) for i in range(POS)]
CY_SWAP = [(i, i ^ 3) for i in range(POS)]
Z_RING = [(i, (i + 4) % POS) for i in range(POS)]
CHIP_UP = [(i, i + 2) for i in range(POS - 2)]
CHIP_DOWN = [(i + 2, i) for i in range(POS - 2)]
X_SWAP = [(0, 1), (1, 0)]


def over_pos(pairs):
    return lambda v: lax.ppermute(v, "pos", pairs)


c_swap, y_swap, cy_swap = over_pos(C_SWAP), over_pos(Y_SWAP), over_pos(CY_SWAP)
z_ring = over_pos(Z_RING)


def x_swap(v):
    return lax.ppermute(v, "group", X_SWAP)


def project_kernel(idx, acts, gain, wq, wk, wv, *outs):
    a = acts[...].astype(F32)
    centre = a - jnp.mean(a, axis=-1, keepdims=True)
    normed = (
        centre * lax.rsqrt(jnp.mean(centre * centre, axis=-1, keepdims=True) + 1e-05) * gain[...]
    ).astype(BF16)
    q = (jnp.dot(normed, wq[...], preferred_element_type=F32) * HK ** (-0.5))
    k = jnp.dot(normed, wk[...], preferred_element_type=F32)
    v = jnp.dot(normed, wv[...], preferred_element_type=F32)
    zeros = jnp.zeros((a.shape[0], HK), F32)
    packs = []
    for h in range(HEADS):
        packs.append(
            jnp.concatenate(
                [
                    v[:, HV * h : HV * (h + 1)],
                    k[:, HK * h : HK * (h + 1)],
                    zeros,
                    q[:, HK * h : HK * (h + 1)],
                ],
                axis=1,
            ).astype(BF16)
        )
    mine = 2 * idx[1] + idx[3]
    for h in range(HEADS):
        for s in range(HEADS):

            @pl.when((mine ^ s) == h)
            def _():
                outs[s][...] = packs[h]


def project(idx, acts, gain, wq, wk, wv):
    rows = acts.shape[0]
    return pl.pallas_call(
        project_kernel,
        out_shape=[jax.ShapeDtypeStruct((rows, 384), BF16)] * HEADS,
        in_specs=[SMEM] + [VMEM] * 5,
        out_specs=[VMEM] * HEADS,
        compiler_params=LIMIT,
        name="project",
    )(idx, acts, gain, wq, wk, wv)


def attend_kernel(*refs):
    packs, kvs, outs = refs[:4], refs[4:8], refs[8:]
    for s in range(2):
        rows = pl.ds(64 * s, 64)
        query = jnp.concatenate([p[rows, 256:384] for p in packs], axis=0)
        query = jnp.concatenate([jnp.zeros_like(query), query], axis=1)
        kv = jnp.concatenate([r[pl.ds(256 * s, 256), :] for r in kvs], axis=0)
        scores = lax.dot_general(
            query, kv, (((1,), (1,)), ((), ())), preferred_element_type=F32
        )
        weights = jnp.exp(scores - jnp.max(scores, axis=-1, keepdims=True))
        total = jnp.sum(weights, axis=-1, keepdims=True)
        mixed = (
            jnp.dot(weights.astype(BF16), kv, preferred_element_type=F32) / total
        ).astype(BF16)
        for j in range(4):
            outs[j][rows, :] = mixed[64 * j : 64 * (j + 1), :]


def attend(packs, kvs):
    return pl.pallas_call(
        attend_kernel,
        out_shape=[jax.ShapeDtypeStruct((128, 256), BF16)] * 4,
        in_specs=[VMEM] * 8,
        out_specs=[VMEM] * 4,
        compiler_params=LIMIT,
        name="attend",
    )(*packs, *kvs)


def output_kernel(idx, acts, wo, *refs):
    mixed, out = refs[:4], refs[4]
    mine = 2 * idx[1] + idx[3]
    total = acts[...].astype(F32)
    summed = None
    for s in range(4):
        rows = pl.ds(pl.multiple_of((mine ^ s) * HV, HV), HV)
        term = jnp.dot(mixed[s][:, :HV], wo[rows, :], preferred_element_type=F32)
        summed = term if summed is None else summed + term
    attended = (total + summed).astype(BF16).astype(F32)
    out[...] = jax.nn.gelu(attended).astype(BF16)


def output(idx, acts, wo, mixed):
    return pl.pallas_call(
        output_kernel,
        out_shape=jax.ShapeDtypeStruct(acts.shape, BF16),
        in_specs=[SMEM] + [VMEM] * 6,
        out_specs=VMEM,
        compiler_params=LIMIT,
        name="output",
    )(idx, acts, wo, *mixed)


def start_all(copies, sems):
    started = []
    for n, (src, dst) in enumerate(copies):
        copy = pltpu.make_async_copy(src, dst, sems.at[n])
        copy.start()
        started.append(copy)
    return started


def place(ref, blocks, columns, dst, height, pos, col):
    return [
        (
            ref.at[pl.ds(row, height), columns],
            dst.at[pl.ds(pl.multiple_of(p * height, height), height), col],
        )
        for row, p in zip(blocks, pos)
    ]


ALL = slice(None)


def quarter(x):
    return pl.ds(pl.multiple_of(x * 384, 384), 384)


def merge_kernel(idx, act_own, act_oth, skip_own, skip_oth, *refs):
    pieces, (merged, first, last), (wl, ws, act, skip, sems) = refs[:14], refs[14:17], refs[17:]
    x, y, z, c = idx[0], idx[1], idx[2], idx[3]
    copies = []

    def add(ref, zz, yy, col):
        pos = [4 * zz + 2 * yy + c, 4 * zz + 2 * yy + 1 - c]
        copies.extend(place(ref, (0, 176), ALL, wl, 96, pos, col))
        copies.extend(place(ref, (96, 272), ALL, ws, 80, pos, col))

    own, yown = pieces[:2]
    add(own, z, y, ALL)
    add(yown, z, 1 - y, ALL)
    for k in range(1, 4):
        zz = lax.rem(z + 4 - k, 4)
        a, b, xa, xb = pieces[2 + 4 * (k - 1) : 2 + 4 * k]
        add(a, zz, y, quarter(x))
        add(b, zz, 1 - y, quarter(x))
        add(xa, zz, y, quarter(1 - x))
        add(xb, zz, 1 - y, quarter(1 - x))
    started = start_all(copies, sems)
    for s in range(2):
        for src_a, src_s, cc in ((act_own, skip_own, c), (act_oth, skip_oth, 1 - c)):
            act[pl.ds(pl.multiple_of(128 * s + 64 * cc, 64), 64), :] = src_a[
                pl.ds(64 * s, 64), :
            ]
            skip[pl.ds(pl.multiple_of(256 * s + 128 * cc, 128), 128), :] = src_s[
                pl.ds(128 * s, 128), :
            ]
    twice = (
        lax.broadcasted_iota(jnp.int32, (256, 128), 0) // 2
        == lax.broadcasted_iota(jnp.int32, (256, 128), 1)
    ).astype(BF16)
    for copy in started:
        copy.wait()
    lifted = jnp.dot(act[...], wl[...], preferred_element_type=F32).astype(BF16)
    for s in range(2):
        term = jnp.dot(
            skip[pl.ds(256 * s, 256), :], ws[...], preferred_element_type=F32
        )
        raised = jnp.dot(twice, lifted[128 * s : 128 * (s + 1)], preferred_element_type=F32)
        total = (raised + term).astype(BF16)
        merged[s, :, :] = total
        first[s : s + 1, :] = total[0:1, :]
        last[s : s + 1, :] = total[255:256, :]


def merge(idx, act_own, act_oth, skip_own, skip_oth, pieces):
    return pl.pallas_call(
        merge_kernel,
        out_shape=[
            jax.ShapeDtypeStruct((2, 256, 768), BF16),
            jax.ShapeDtypeStruct((2, 768), BF16),
            jax.ShapeDtypeStruct((2, 768), BF16),
        ],
        in_specs=[SMEM] + [VMEM] * 4 + [ANY] * len(pieces),
        out_specs=[VMEM] * 3,
        scratch_shapes=[
            pltpu.VMEM((1536, 768), BF16),
            pltpu.VMEM((1280, 768), BF16),
            pltpu.VMEM((256, 1536), BF16),
            pltpu.VMEM((512, 1280), BF16),
            pltpu.SemaphoreType.DMA((56,)),
        ],
        compiler_params=LIMIT,
        name="merge",
    )(idx, act_own, act_oth, skip_own, skip_oth, *pieces)


def point_kernel(idx, depth, merged, before, after, *refs):
    pieces, (own, oth), (wp, spread, sems) = refs[:9], refs[9:11], refs[11:]
    x, y, z, c = idx[0], idx[1], idx[2], idx[3]
    copies = []

    def add(ref, zz, yy, col, row=0):
        pos = [4 * zz + 2 * yy + c, 4 * zz + 2 * yy + 1 - c]
        copies.extend(place(ref, (row, row + 96), ALL, wp, 96, pos, col))

    add(pieces[0], z, y, ALL)
    add(pieces[1], z, 1 - y, quarter(x))
    add(pieces[2], z, 1 - y, quarter(1 - x))
    for k in range(1, 4):
        zz = lax.rem(z + 4 - k, 4)
        for ref, col in ((pieces[2 * k + 1], quarter(x)), (pieces[2 * k + 2], quarter(1 - x))):
            add(ref, zz, y, col)
            add(ref, zz, 1 - y, col, 192)
    started = start_all(copies, sems)
    taps = depth[:, pl.ds(pl.multiple_of(c * 768, 768), 768)]
    row = lax.broadcasted_iota(jnp.int32, (256, 768), 0)
    for s in range(2):
        here = merged[s, :, :].astype(F32)
        up = jnp.where(row == 0, before[s : s + 1, :].astype(F32), pltpu.roll(here, 1, 0))
        down = jnp.where(row == 255, after[s : s + 1, :].astype(F32), pltpu.roll(here, 255, 0))
        spread[pl.ds(256 * s, 256), :] = (
            taps[0:1] * up + taps[1:2] * here + taps[2:3] * down
        ).astype(BF16)
    for copy in started:
        copy.wait()
    for s in range(2):
        for out, cc in ((oth, 1 - c), (own, c)):
            part = spread[pl.ds(pl.multiple_of(256 * s + 128 * cc, 128), 128), :]
            out[s, :, :] = lax.dot_general(
                part, wp[...], (((1,), (1,)), ((), ())), preferred_element_type=F32
            ).astype(out.dtype)


def point(idx, depth, merged, before, after, pieces):
    return pl.pallas_call(
        point_kernel,
        out_shape=[
            jax.ShapeDtypeStruct((2, 128, 1536), F32),
            jax.ShapeDtypeStruct((2, 128, 1536), BF16),
        ],
        in_specs=[SMEM] + [VMEM] * 4 + [ANY] * len(pieces),
        out_specs=[VMEM] * 2,
        scratch_shapes=[
            pltpu.VMEM((1536, 768), BF16),
            pltpu.VMEM((512, 768), BF16),
            pltpu.SemaphoreType.DMA((30,)),
        ],
        compiler_params=LIMIT,
        name="point",
    )(idx, depth, merged, before, after, *pieces)


def columns(v, i, width):
    return lax.dynamic_slice_in_dim(v, i * width, width, axis=1)


def on_device(
    acts, skips, norm_gain, w_query, w_key, w_value, w_out, w_lift, w_skip, depth_kernel, w_point
):
    pos = lax.axis_index("pos")
    x, c, y, z = lax.axis_index("group"), pos % 2, pos // 2 % 2, pos // 4
    idx = jnp.stack([x, y, z, c]).astype(jnp.int32)
    flat = acts.reshape(128, 1536)

    def chip_half(shard):
        return jnp.concatenate(
            [columns(shard, c, 768), c_swap(columns(shard, 1 - c, 768))], axis=0
        )

    half_a = chip_half(jnp.concatenate([w_lift, w_skip], axis=0))
    half_b = chip_half(w_point.T)
    pieces_a = [half_a, y_swap(half_a)]
    a = columns(half_a, x, 384)
    for _ in range(3):
        a = z_ring(a)
        b = y_swap(a)
        pieces_a += [a, b, x_swap(a), x_swap(b)]
    mine_b = columns(half_b, x, 384)
    y_mine_b = y_swap(mine_b)
    pieces_b = [half_b, y_mine_b, y_swap(columns(half_b, 1 - x, 384))]
    b = jnp.concatenate([mine_b, y_mine_b], axis=0)
    for _ in range(3):
        b = z_ring(b)
        pieces_b += [b, x_swap(b)]

    packs = project(idx, flat, norm_gain.reshape(1, -1), w_query, w_key, w_value)
    swaps = [lambda v: v, c_swap, y_swap, cy_swap]
    packs = [swap(p) for swap, p in zip(swaps, packs)]
    kv = jnp.concatenate(
        [p[:, :256].reshape(2, 64, 256) for p in packs], axis=1
    ).reshape(512, 256)
    kvs = [kv]
    for _ in range(3):
        kv = z_ring(kv)
        kvs.append(kv)
    mixed = attend(packs, kvs)
    mixed = [swap(m) for swap, m in zip(swaps, mixed)]
    activated = output(idx, flat, w_out, mixed)
    skip_act = jax.nn.gelu(skips.astype(F32)).astype(BF16).reshape(256, 1280)
    merged, first, last = merge(
        idx, activated, c_swap(activated), skip_act, c_swap(skip_act), pieces_a
    )
    before = lax.ppermute(last, "pos", CHIP_UP)
    after = lax.ppermute(first, "pos", CHIP_DOWN)
    own, oth = point(idx, depth_kernel, merged, before, after, pieces_b)
    return (own + c_swap(oth).astype(F32)).astype(BF16)


def extended(cells, sides, width):
    for axis, dim in sides:
        count = lax.axis_size(axis)
        ends = count - 1
        head = lax.slice_in_dim(cells, 0, width, axis=dim)
        tail = lax.slice_in_dim(cells, cells.shape[dim] - width, cells.shape[dim], axis=dim)
        cells = jnp.concatenate(
            [
                lax.ppermute(tail, axis, [(i, (i + 1) % count) for i in range(ends)]),
                cells,
                lax.ppermute(head, axis, [((i + 1) % count, i) for i in range(ends)]),
            ],
            axis=dim,
        )
    return cells


def on_device_plain(
    acts, skips, norm_gain, w_query, w_key, w_value, w_out, w_lift, w_skip, depth_kernel, w_point
):
    lift_full, skip_full, point_full = (
        lax.all_gather(w_lift, "pos", axis=0, tiled=True),
        lax.all_gather(w_skip, "pos", axis=0, tiled=True),
        lax.all_gather(w_point, "pos", axis=1, tiled=True),
    )
    seq_count, bin_rows, width = acts.shape
    actsf = acts.astype(jnp.float32)
    centre = actsf - jnp.mean(actsf, axis=-1, keepdims=True)
    normed = (
        centre * lax.rsqrt(jnp.mean(centre * centre, axis=-1, keepdims=True) + 1e-05) * norm_gain
    ).astype(jnp.bfloat16)
    flat = normed.reshape(seq_count * bin_rows, width)
    queries = (
        (jnp.dot(flat, w_query, preferred_element_type=jnp.float32) * HK ** (-0.5))
        .astype(jnp.bfloat16)
        .reshape(seq_count, bin_rows, HEADS, HK)
    )
    keys_here = (
        jnp.dot(flat, w_key, preferred_element_type=jnp.float32)
        .astype(jnp.bfloat16)
        .reshape(seq_count, bin_rows, HEADS * HK)
    )
    values_here = (
        jnp.dot(flat, w_value, preferred_element_type=jnp.float32)
        .astype(jnp.bfloat16)
        .reshape(seq_count, bin_rows, HEADS * HV)
    )
    running = jnp.full((seq_count, HEADS, bin_rows), -1e30, jnp.float32)
    key_piece = lax.all_gather(keys_here, "pos", axis=1, tiled=True)
    value_piece = lax.all_gather(values_here, "pos", axis=1, tiled=True)
    count = key_piece.shape[1]
    keyed = key_piece.reshape(seq_count, count, HEADS, HK)
    valued = value_piece.reshape(seq_count, count, HEADS, HV)
    scores = jnp.einsum("sqhd,skhd->shqk", queries, keyed, preferred_element_type=jnp.float32)
    newest = jnp.maximum(running, jnp.max(scores, axis=-1))
    weights = jnp.exp(scores - newest[..., None])
    totals = jnp.sum(weights, axis=-1)
    summed = jnp.einsum(
        "shqk,skhv->shqv", weights.astype(jnp.bfloat16), valued, preferred_element_type=jnp.float32
    )
    running, totals, summed = (newest, totals, summed)
    mixed = (
        (summed / totals[..., None])
        .transpose(0, 2, 1, 3)
        .reshape(seq_count * bin_rows, HEADS * HV)
        .astype(jnp.bfloat16)
    )
    attended = (
        actsf.reshape(seq_count * bin_rows, width)
        + jnp.dot(mixed, w_out, preferred_element_type=jnp.float32)
    ).astype(jnp.bfloat16)
    activated = jax.nn.gelu(attended.astype(jnp.float32)).astype(jnp.bfloat16)
    lifted = jnp.dot(activated, lift_full, preferred_element_type=jnp.float32)
    lifted = lifted.astype(jnp.bfloat16).reshape(seq_count, bin_rows, width)
    raised = jnp.repeat(lifted, 2, axis=1).reshape(seq_count * 2 * bin_rows, width)
    skip_act = (
        jax.nn.gelu(skips.astype(jnp.float32))
        .astype(jnp.bfloat16)
        .reshape(seq_count * 2 * bin_rows, skips.shape[2])
    )
    skip_term = jnp.dot(skip_act, skip_full, preferred_element_type=jnp.float32)
    merged = (
        (raised.astype(jnp.float32) + skip_term)
        .astype(jnp.bfloat16)
        .reshape(seq_count, 2 * bin_rows, width)
    )
    padded = extended(merged, (("pos", 1),), 1)
    paddedf = padded.astype(jnp.float32)
    spread = (
        depth_kernel[0] * paddedf[:, :-2]
        + depth_kernel[1] * paddedf[:, 1:-1]
        + depth_kernel[2] * paddedf[:, 2:]
    ).astype(jnp.bfloat16)
    spread = spread.reshape(seq_count * 2 * bin_rows, width)
    decoded = jnp.dot(spread, point_full, preferred_element_type=jnp.float32)
    return decoded.astype(jnp.bfloat16).reshape(seq_count, 2 * bin_rows, width)


def solution(mesh):
    planned = dict(mesh.shape) == {"group": 2, "pos": POS}
    return jax.shard_map(
        on_device if planned else on_device_plain,
        mesh=mesh,
        in_specs=(
            P("group", "pos", None),
            P("group", "pos", None),
            P(),
            P(),
            P(),
            P(),
            P(),
            P("pos", None),
            P("pos", None),
            P(),
            P(None, "pos"),
        ),
        out_specs=P("group", "pos", None),
        check_vma=False,
    )
```

```python
import functools

import jax
import jax.numpy as jnp
from jax import lax
from jax.experimental import pallas as pl
from jax.experimental.pallas import tpu as pltpu
from jax.sharding import PartitionSpec as P

HEADS = 4
HK = 64
HV = 192
F32 = jnp.float32
BF16 = jnp.bfloat16
ANY = pl.BlockSpec(memory_space=pl.ANY)
VMEM = pl.BlockSpec(memory_space=pltpu.VMEM)
HBM = pl.BlockSpec(memory_space=pltpu.HBM)
SMEM = pl.BlockSpec(memory_space=pltpu.SMEM)
LIMIT = pltpu.CompilerParams(vmem_limit_bytes=20 * 1024 * 1024)

WIDTH = 5
CUMULATIVE = False
SENDS = (
    ("u1", "z", "u0"),
    ("qy", "y", "py"),
    ("qcy", "cy", "pcy"),
    ("qc", "c", "pc"),
    ("k1", "z", "k0"),
    ("b1", "y", "u1"),
    ("u2", "z", "u1"),
    ("c1", "x", "u1"),
    ("b0", "y", "u0"),
    ("skipc", "c", "skip"),
    ("k2", "z", "k1"),
    ("d1", "x", "b1"),
    ("c2", "x", "u2"),
    ("b2", "y", "u2"),
    ("u3", "z", "u2"),
    ("k3", "z", "k2"),
    ("d2", "x", "b2"),
    ("b3", "y", "u3"),
    ("mc", "c", "oc"),
    ("my", "y", "oy"),
    ("mcy", "cy", "ocy"),
    ("c3", "z", "c2"),
    ("d0", "y", "c0"),
    ("actc", "c", "act"),
    ("before", "up", "high"),
    ("after", "down", "low"),
    ("d3", "x", "b3"),
)

POS = 16
C_SWAP = [(i, i ^ 1) for i in range(POS)]
Y_SWAP = [(i, i ^ 2) for i in range(POS)]
CY_SWAP = [(i, i ^ 3) for i in range(POS)]
Z_RING = [(i, (i + 4) % POS) for i in range(POS)]
CHIP_UP = [(i, i + 2) for i in range(POS - 2)]
CHIP_DOWN = [(i + 2, i) for i in range(POS - 2)]
X_SWAP = [(0, 1), (1, 0)]


def over_pos(pairs):
    return lambda v: lax.ppermute(v, "pos", pairs)


c_swap, y_swap, cy_swap = over_pos(C_SWAP), over_pos(Y_SWAP), over_pos(CY_SWAP)
z_ring = over_pos(Z_RING)


def x_swap(v):
    return lax.ppermute(v, "group", X_SWAP)


def project_kernel(idx, acts_hbm, gain, wq_hbm, wk_hbm, wv_hbm, *refs):
    outs, (acts, wq, wk, wv, sems) = refs[:4], refs[4:]
    copies = [
        pltpu.make_async_copy(src, dst, sems.at[n])
        for n, (src, dst) in enumerate(
            ((acts_hbm, acts), (wq_hbm, wq), (wk_hbm, wk), (wv_hbm, wv))
        )
    ]
    for copy in copies:
        copy.start()
    copies.pop(0).wait()
    a = acts[...].astype(F32)
    centre = a - jnp.mean(a, axis=-1, keepdims=True)
    normed = (
        centre * lax.rsqrt(jnp.mean(centre * centre, axis=-1, keepdims=True) + 1e-05) * gain[...]
    ).astype(BF16)
    for copy in copies:
        copy.wait()
    q = (jnp.dot(normed, wq[...], preferred_element_type=F32) * HK ** (-0.5))
    k = jnp.dot(normed, wk[...], preferred_element_type=F32)
    v = jnp.dot(normed, wv[...], preferred_element_type=F32)
    zeros = jnp.zeros((a.shape[0], HK), F32)
    packs = []
    for h in range(HEADS):
        packs.append(
            jnp.concatenate(
                [
                    v[:, HV * h : HV * (h + 1)],
                    k[:, HK * h : HK * (h + 1)],
                    zeros,
                    q[:, HK * h : HK * (h + 1)],
                ],
                axis=1,
            ).astype(BF16)
        )
    mine = 2 * idx[1] + idx[3]
    for h in range(HEADS):
        for s in range(HEADS):

            @pl.when((mine ^ s) == h)
            def _():
                outs[s][...] = packs[h]


def project(idx, acts, gain, wq, wk, wv):
    rows = acts.shape[0]
    return pl.pallas_call(
        project_kernel,
        out_shape=[jax.ShapeDtypeStruct((rows, 384), BF16)] * HEADS,
        in_specs=[SMEM, HBM, VMEM] + [HBM] * 3,
        out_specs=[VMEM] * HEADS,
        scratch_shapes=[
            pltpu.VMEM((128, 1536), BF16),
            pltpu.VMEM((1536, 256), BF16),
            pltpu.VMEM((1536, 256), BF16),
            pltpu.VMEM((1536, 768), BF16),
            pltpu.SemaphoreType.DMA((4,)),
        ],
        compiler_params=LIMIT,
        name="project",
    )(idx, acts, gain, wq, wk, wv)


def attend_kernel(*refs):
    packs, kvs, outs = refs[:4], refs[4:8], refs[8:]
    for s in range(2):
        rows = pl.ds(64 * s, 64)
        query = jnp.concatenate([p[rows, 256:384] for p in packs], axis=0)
        query = jnp.concatenate([jnp.zeros_like(query), query], axis=1)
        kv = jnp.concatenate([r[pl.ds(256 * s, 256), :] for r in kvs], axis=0)
        scores = lax.dot_general(
            query, kv, (((1,), (1,)), ((), ())), preferred_element_type=F32
        )
        weights = jnp.exp(scores - jnp.max(scores, axis=-1, keepdims=True))
        total = jnp.sum(weights, axis=-1, keepdims=True)
        mixed = (
            jnp.dot(weights.astype(BF16), kv, preferred_element_type=F32) / total
        ).astype(BF16)
        for j in range(4):
            outs[j][rows, :] = mixed[64 * j : 64 * (j + 1), :]


def attend(packs, kvs):
    return pl.pallas_call(
        attend_kernel,
        out_shape=[jax.ShapeDtypeStruct((128, 256), BF16)] * 4,
        in_specs=[VMEM] * 8,
        out_specs=[VMEM] * 4,
        compiler_params=LIMIT,
        name="attend",
    )(*packs, *kvs)


def output_kernel(idx, acts, wo, *refs):
    mixed, out = refs[:4], refs[4]
    mine = 2 * idx[1] + idx[3]
    total = acts[...].astype(F32)
    summed = None
    for s in range(4):
        rows = pl.ds(pl.multiple_of((mine ^ s) * HV, HV), HV)
        term = jnp.dot(mixed[s][:, :HV], wo[rows, :], preferred_element_type=F32)
        summed = term if summed is None else summed + term
    attended = (total + summed).astype(BF16).astype(F32)
    out[...] = jax.nn.gelu(attended).astype(BF16)


def output(idx, acts, wo, mixed):
    return pl.pallas_call(
        output_kernel,
        out_shape=jax.ShapeDtypeStruct(acts.shape, BF16),
        in_specs=[SMEM] + [VMEM] * 6,
        out_specs=VMEM,
        compiler_params=LIMIT,
        name="output",
    )(idx, acts, wo, *mixed)


ALL = slice(None)


def quarter(x):
    return pl.ds(pl.multiple_of(x * 384, 384), 384)


def rows_of(p, height):
    return pl.ds(pl.multiple_of(p * height, height), height)


A_ROWS = 352


def merge_kernel(idx, act_own, act_oth, skip_own, skip_oth, before, after, *refs):
    pieces, (merged, ends), (wl, ws, act, skip) = refs[:15], refs[15:17], refs[17:]
    x, y, z, c = idx[0], idx[1], idx[2], idx[3]

    def add(ref, zz, yy, col):
        for n, cc in ((0, c), (176, 1 - c)):
            p = 4 * zz + 2 * yy + cc
            wl[rows_of(p, 96), col] = ref[n : n + 96, :]
            ws[rows_of(p, 80), col] = ref[n + 96 : n + 176, :]

    own, b0, xb0 = pieces[:3]
    add(own, z, y, ALL)
    add(b0, z, 1 - y, quarter(x))
    add(xb0, z, 1 - y, quarter(1 - x))
    for k in range(1, 4):
        zz = lax.rem(z + 4 - k, 4)
        a, b, xa, xb = pieces[4 * k - 1 : 4 * k + 3]
        add(a, zz, y, quarter(x))
        add(b, zz, 1 - y, quarter(x))
        add(xa, zz, y, quarter(1 - x))
        add(xb, zz, 1 - y, quarter(1 - x))
    for s in range(2):
        for src_a, src_s, cc in ((act_own, skip_own, c), (act_oth, skip_oth, 1 - c)):
            act[pl.ds(pl.multiple_of(128 * s + 64 * cc, 64), 64), :] = src_a[
                pl.ds(64 * s, 64), :
            ]
            skip[pl.ds(pl.multiple_of(256 * s + 128 * cc, 128), 128), :] = src_s[
                pl.ds(128 * s, 128), :
            ]
    act[256:272, :] = jnp.concatenate(
        [before[:, :1536], after[:, :1536], jnp.zeros((12, 1536), BF16)], axis=0
    )
    skip[512:528, :] = jnp.concatenate(
        [before[:, 1536:], after[:, 1536:], jnp.zeros((12, 1280), BF16)], axis=0
    )
    twice = (
        lax.broadcasted_iota(jnp.int32, (256, 128), 0) // 2
        == lax.broadcasted_iota(jnp.int32, (256, 128), 1)
    ).astype(BF16)
    lifted = jnp.dot(act[...], wl[...], preferred_element_type=F32).astype(BF16)
    terms = jnp.dot(skip[...], ws[...], preferred_element_type=F32)
    for s in range(2):
        term = terms[256 * s : 256 * (s + 1)]
        raised = jnp.dot(twice, lifted[128 * s : 128 * (s + 1)], preferred_element_type=F32)
        total = (raised + term).astype(BF16)
        merged[s, :, :] = total
    ends[...] = (lifted[256:272].astype(F32) + terms[512:528]).astype(BF16)


def merge(idx, act_own, act_oth, skip_own, skip_oth, before, after, pieces):
    return pl.pallas_call(
        merge_kernel,
        out_shape=[
            jax.ShapeDtypeStruct((2, 256, 768), BF16),
            jax.ShapeDtypeStruct((16, 768), BF16),
        ],
        in_specs=[SMEM] + [VMEM] * (6 + len(pieces)),
        out_specs=[VMEM] * 2,
        scratch_shapes=[
            pltpu.VMEM((1536, 768), BF16),
            pltpu.VMEM((1280, 768), BF16),
            pltpu.VMEM((272, 1536), BF16),
            pltpu.VMEM((528, 1280), BF16),
        ],
        compiler_params=LIMIT,
        name="merge",
    )(idx, act_own, act_oth, skip_own, skip_oth, before, after, *pieces)


def point_kernel(idx, depth, merged, ends, *refs):
    pieces, (own, oth), (wp, spread) = refs[:15], refs[15:17], refs[17:]
    x, y, z, c = idx[0], idx[1], idx[2], idx[3]

    def add(ref, zz, yy, col):
        base = A_ROWS
        for n, cc in ((base, c), (base + 96, 1 - c)):
            wp[rows_of(4 * zz + 2 * yy + cc, 96), col] = ref[n : n + 96, :]

    full, b0, xb0 = pieces[:3]
    add(full, z, y, ALL)
    add(b0, z, 1 - y, quarter(x))
    add(xb0, z, 1 - y, quarter(1 - x))
    for k in range(1, 4):
        zz = lax.rem(z + 4 - k, 4)
        a, b, xa, xb = pieces[4 * k - 1 : 4 * k + 3]
        add(a, zz, y, quarter(x))
        add(b, zz, 1 - y, quarter(x))
        add(xa, zz, y, quarter(1 - x))
        add(xb, zz, 1 - y, quarter(1 - x))
    taps = depth[:, pl.ds(pl.multiple_of(c * 768, 768), 768)]
    row = lax.broadcasted_iota(jnp.int32, (256, 768), 0)
    for s in range(2):
        here = merged[s, :, :].astype(F32)
        up = jnp.where(row == 0, ends[s : s + 1, :].astype(F32), pltpu.roll(here, 1, 0))
        down = jnp.where(row == 255, ends[s + 2 : s + 3, :].astype(F32), pltpu.roll(here, 255, 0))
        spread[pl.ds(256 * s, 256), :] = (
            taps[0:1] * up + taps[1:2] * here + taps[2:3] * down
        ).astype(BF16)
    for out, cc in ((oth, 1 - c), (own, c)):
        part = jnp.concatenate(
            [
                spread[pl.ds(pl.multiple_of(256 * s + 128 * cc, 128), 128), :]
                for s in range(2)
            ],
            axis=0,
        )
        out[...] = (
            lax.dot_general(part, wp[...], (((1,), (1,)), ((), ())), preferred_element_type=F32)
            .astype(out.dtype)
            .reshape(out.shape)
        )


def point(idx, depth, merged, ends, pieces):
    return pl.pallas_call(
        point_kernel,
        out_shape=[
            jax.ShapeDtypeStruct((2, 128, 1536), F32),
            jax.ShapeDtypeStruct((2, 128, 1536), BF16),
        ],
        in_specs=[SMEM] + [VMEM] * (3 + len(pieces)),
        out_specs=[VMEM] * 2,
        scratch_shapes=[
            pltpu.VMEM((1536, 768), BF16),
            pltpu.VMEM((512, 768), BF16),
        ],
        compiler_params=LIMIT,
        name="point",
    )(idx, depth, merged, ends, *pieces)


def behind(v, *tokens):
    return lax.optimization_barrier((v,) + tokens)[0]


class Plan:
    def __init__(self, width, makers):
        self.width, self.makers, self.made, self.done = width, makers, {}, []

    def __getitem__(self, name):
        if name not in self.made:
            self.made[name] = self.makers[name]()
        return self.made[name]

    def send(self, how, name):
        v = self[name]
        if len(self.done) >= self.width:
            late = self.done[: len(self.done) - self.width + 1]
            v = behind(v, *(late if CUMULATIVE else late[-1:]))
        got = how(v)
        if how is not c_swap:
            self.done.append(got)
        return got


def in_hbm(v):
    return pltpu.with_memory_space_constraint(v, pltpu.HBM)


def split_kernel(idx, wl, ws, wp, keep, send, sems):
    c = idx[3]
    copies = []
    for out, cc in ((send, 1 - c), (keep, c)):
        cols = pl.ds(pl.multiple_of(768 * cc, 768), 768)
        for src, lo, hi in ((wl, 0, 96), (ws, 96, 176), (wp, 176, 272)):
            copies.append(
                pltpu.make_async_copy(src.at[:, cols], out.at[lo:hi], sems.at[len(copies)])
            )
    for copy in copies:
        copy.start()
    for copy in copies:
        copy.wait()


def split(idx, wl, ws, wp):
    return pl.pallas_call(
        split_kernel,
        out_shape=[jax.ShapeDtypeStruct((272, 768), BF16)] * 2,
        in_specs=[SMEM] + [HBM] * 3,
        out_specs=[VMEM] * 2,
        scratch_shapes=[
            pltpu.SemaphoreType.DMA((6,)),
        ],
        compiler_params=LIMIT,
        name="split",
    )(idx, wl, ws, wp)


def join_kernel(idx, keep, got, full, quart, rest):
    x = idx[0]
    for n, ref in enumerate((keep, got)):
        for dst, src in (
            (slice(176 * n, 176 * (n + 1)), slice(0, 176)),
            (slice(352 + 96 * n, 352 + 96 * (n + 1)), slice(176, 272)),
        ):
            full[dst, :] = ref[src, :]
            quart[dst, :] = ref[src, quarter(x)]
            rest[dst, :] = ref[src, quarter(1 - x)]


def join(idx, keep, got):
    return pl.pallas_call(
        join_kernel,
        out_shape=[
            jax.ShapeDtypeStruct(shape, BF16) for shape in ((544, 768), (544, 384), (544, 384))
        ],
        in_specs=[SMEM] + [VMEM] * 2,
        out_specs=[VMEM] * 3,
        compiler_params=LIMIT,
        name="join",
    )(idx, keep, got)


def edges_kernel(idx, act_own, act_oth, skip_own, skip_oth, low, high):
    c = idx[3]
    for first, last, mine in (
        ((act_own, skip_own), (act_oth, skip_oth), 0),
        ((act_oth, skip_oth), (act_own, skip_own), 1),
    ):

        @pl.when(c == mine)
        def _():
            for s in range(2):
                for cols, n, rows in ((slice(0, 1536), 0, 64), (slice(1536, 2816), 1, 128)):
                    low[s : s + 1, cols] = first[n][rows * s : rows * s + 1, :]
                    end = rows * (s + 1)
                    high[s : s + 1, cols] = last[n][end - 1 : end, :]


def edges(idx, act_own, act_oth, skip_own, skip_oth):
    return pl.pallas_call(
        edges_kernel,
        out_shape=[jax.ShapeDtypeStruct((2, 2816), BF16)] * 2,
        in_specs=[SMEM] + [VMEM] * 4,
        out_specs=[VMEM] * 2,
        compiler_params=LIMIT,
        name="edges",
    )(idx, act_own, act_oth, skip_own, skip_oth)


def on_device(
    acts, skips, norm_gain, w_query, w_key, w_value, w_out, w_lift, w_skip, depth_kernel, w_point
):
    pos = lax.axis_index("pos")
    x, c, y, z = lax.axis_index("group"), pos % 2, pos // 2 % 2, pos // 4
    idx = jnp.stack([x, y, z, c]).astype(jnp.int32)
    flat = acts.reshape(128, 1536)
    keep, send = split(idx, *map(in_hbm, (w_lift, w_skip, w_point.T)))
    full, u0, c0 = join(idx, keep, c_swap(send))

    def projected():
        return project(
            idx,
            in_hbm(behind(flat, u0)),
            norm_gain.reshape(1, -1),
            *map(in_hbm, (w_query, w_key, w_value)),
        )

    def joined():
        packs = [plan[n] for n in ("q0", "qc", "qy", "qcy")]
        return jnp.concatenate(
            [p[:, :256].reshape(2, 64, 256) for p in packs], axis=1
        ).reshape(512, 256)

    def attended():
        return attend(
            [plan[n] for n in ("q0", "qc", "qy", "qcy")],
            [plan[n] for n in ("k0", "k1", "k2", "k3")],
        )

    makers = {
        "u0": lambda: u0,
        "c0": lambda: c0,
        "packs": projected,
        "k0": joined,
        "mixes": attended,
        "act": lambda: output(idx, flat, w_out, [plan[n] for n in ("m0", "mc", "my", "mcy")]),
        "skip": lambda: jax.nn.gelu(skips.astype(F32)).astype(BF16).reshape(256, 1280),
        "edges": lambda: edges(idx, *(plan[n] for n in ("act", "actc", "skip", "skipc"))),
        "low": lambda: plan["edges"][0],
        "high": lambda: plan["edges"][1],
    }
    for n, way in enumerate(("0", "c", "y", "cy")):
        makers["p" + way] = lambda n=n: plan["packs"][n]
        makers["o" + way] = lambda n=n: plan["mixes"][n]
    makers["q0"], makers["m0"] = makers["p0"], makers["o0"]
    swaps = {"c": c_swap, "y": y_swap, "cy": cy_swap, "x": x_swap, "z": z_ring}
    swaps |= {"up": over_pos(CHIP_UP), "down": over_pos(CHIP_DOWN)}

    def sender(how, src):
        return lambda: plan.send(swaps[how], src)

    for name, how, src in SENDS:
        makers[name] = sender(how, src)
    plan = Plan(WIDTH, makers)
    for name, _, _ in SENDS:
        plan[name]
    pieces = [full, plan["b0"], plan["d0"]] + [
        plan[part + str(k)] for k in (1, 2, 3) for part in "ubcd"
    ]
    merged, ends = merge(
        idx, plan["act"], plan["actc"], plan["skip"], plan["skipc"], plan["before"],
        plan["after"], pieces,
    )
    own, oth = point(idx, depth_kernel, merged, ends, pieces)
    return (own + c_swap(oth).astype(F32)).astype(BF16)


def extended(cells, sides, width):
    for axis, dim in sides:
        count = lax.axis_size(axis)
        ends = count - 1
        head = lax.slice_in_dim(cells, 0, width, axis=dim)
        tail = lax.slice_in_dim(cells, cells.shape[dim] - width, cells.shape[dim], axis=dim)
        cells = jnp.concatenate(
            [
                lax.ppermute(tail, axis, [(i, (i + 1) % count) for i in range(ends)]),
                cells,
                lax.ppermute(head, axis, [((i + 1) % count, i) for i in range(ends)]),
            ],
            axis=dim,
        )
    return cells


def on_device_plain(
    acts, skips, norm_gain, w_query, w_key, w_value, w_out, w_lift, w_skip, depth_kernel, w_point
):
    lift_full, skip_full, point_full = (
        lax.all_gather(w_lift, "pos", axis=0, tiled=True),
        lax.all_gather(w_skip, "pos", axis=0, tiled=True),
        lax.all_gather(w_point, "pos", axis=1, tiled=True),
    )
    seq_count, bin_rows, width = acts.shape
    actsf = acts.astype(jnp.float32)
    centre = actsf - jnp.mean(actsf, axis=-1, keepdims=True)
    normed = (
        centre * lax.rsqrt(jnp.mean(centre * centre, axis=-1, keepdims=True) + 1e-05) * norm_gain
    ).astype(jnp.bfloat16)
    flat = normed.reshape(seq_count * bin_rows, width)
    queries = (
        (jnp.dot(flat, w_query, preferred_element_type=jnp.float32) * HK ** (-0.5))
        .astype(jnp.bfloat16)
        .reshape(seq_count, bin_rows, HEADS, HK)
    )
    keys_here = (
        jnp.dot(flat, w_key, preferred_element_type=jnp.float32)
        .astype(jnp.bfloat16)
        .reshape(seq_count, bin_rows, HEADS * HK)
    )
    values_here = (
        jnp.dot(flat, w_value, preferred_element_type=jnp.float32)
        .astype(jnp.bfloat16)
        .reshape(seq_count, bin_rows, HEADS * HV)
    )
    running = jnp.full((seq_count, HEADS, bin_rows), -1e30, jnp.float32)
    key_piece = lax.all_gather(keys_here, "pos", axis=1, tiled=True)
    value_piece = lax.all_gather(values_here, "pos", axis=1, tiled=True)
    count = key_piece.shape[1]
    keyed = key_piece.reshape(seq_count, count, HEADS, HK)
    valued = value_piece.reshape(seq_count, count, HEADS, HV)
    scores = jnp.einsum("sqhd,skhd->shqk", queries, keyed, preferred_element_type=jnp.float32)
    newest = jnp.maximum(running, jnp.max(scores, axis=-1))
    weights = jnp.exp(scores - newest[..., None])
    totals = jnp.sum(weights, axis=-1)
    summed = jnp.einsum(
        "shqk,skhv->shqv", weights.astype(jnp.bfloat16), valued, preferred_element_type=jnp.float32
    )
    running, totals, summed = (newest, totals, summed)
    mixed = (
        (summed / totals[..., None])
        .transpose(0, 2, 1, 3)
        .reshape(seq_count * bin_rows, HEADS * HV)
        .astype(jnp.bfloat16)
    )
    attended = (
        actsf.reshape(seq_count * bin_rows, width)
        + jnp.dot(mixed, w_out, preferred_element_type=jnp.float32)
    ).astype(jnp.bfloat16)
    activated = jax.nn.gelu(attended.astype(jnp.float32)).astype(jnp.bfloat16)
    lifted = jnp.dot(activated, lift_full, preferred_element_type=jnp.float32)
    lifted = lifted.astype(jnp.bfloat16).reshape(seq_count, bin_rows, width)
    raised = jnp.repeat(lifted, 2, axis=1).reshape(seq_count * 2 * bin_rows, width)
    skip_act = (
        jax.nn.gelu(skips.astype(jnp.float32))
        .astype(jnp.bfloat16)
        .reshape(seq_count * 2 * bin_rows, skips.shape[2])
    )
    skip_term = jnp.dot(skip_act, skip_full, preferred_element_type=jnp.float32)
    merged = (
        (raised.astype(jnp.float32) + skip_term)
        .astype(jnp.bfloat16)
        .reshape(seq_count, 2 * bin_rows, width)
    )
    padded = extended(merged, (("pos", 1),), 1)
    paddedf = padded.astype(jnp.float32)
    spread = (
        depth_kernel[0] * paddedf[:, :-2]
        + depth_kernel[1] * paddedf[:, 1:-1]
        + depth_kernel[2] * paddedf[:, 2:]
    ).astype(jnp.bfloat16)
    spread = spread.reshape(seq_count * 2 * bin_rows, width)
    decoded = jnp.dot(spread, point_full, preferred_element_type=jnp.float32)
    return decoded.astype(jnp.bfloat16).reshape(seq_count, 2 * bin_rows, width)


def solution(mesh):
    planned = dict(mesh.shape) == {"group": 2, "pos": POS}
    return jax.shard_map(
        on_device if planned else on_device_plain,
        mesh=mesh,
        in_specs=(
            P("group", "pos", None),
            P("group", "pos", None),
            P(),
            P(),
            P(),
            P(),
            P(),
            P("pos", None),
            P("pos", None),
            P(),
            P(None, "pos"),
        ),
        out_specs=P("group", "pos", None),
        check_vma=False,
    )
```

```python
import functools

import jax
import jax.numpy as jnp
from jax import lax
from jax.experimental import pallas as pl
from jax.experimental.pallas import tpu as pltpu
from jax.sharding import PartitionSpec as P

HEADS = 4
HK = 64
HV = 192
F32 = jnp.float32
BF16 = jnp.bfloat16
ANY = pl.BlockSpec(memory_space=pl.ANY)
VMEM = pl.BlockSpec(memory_space=pltpu.VMEM)
HBM = pl.BlockSpec(memory_space=pltpu.HBM)
SMEM = pl.BlockSpec(memory_space=pltpu.SMEM)
LIMIT = pltpu.CompilerParams(vmem_limit_bytes=20 * 1024 * 1024)

WIDTH = 5
CUMULATIVE = True
SENDS = (
    ("u1", "z", "u0"),
    ("b0", "y", "u0"),
    ("qy", "y", "py"),
    ("u2", "z", "u1"),
    ("c1", "x", "u1"),
    ("qcy", "cy", "pcy"),
    ("b1", "y", "u1"),
    ("k1", "z", "k0"),
    ("c2", "x", "u2"),
    ("b2", "y", "u2"),
    ("u3", "z", "u2"),
    ("qc", "c", "pc"),
    ("k2", "z", "k1"),
    ("skipc", "c", "skip"),
    ("d2", "y", "c2"),
    ("d0", "x", "b0"),
    ("k3", "z", "k2"),
    ("b3", "y", "u3"),
    ("d1", "x", "b1"),
    ("my", "y", "oy"),
    ("mc", "c", "oc"),
    ("mcy", "cy", "ocy"),
    ("c3", "x", "u3"),
    ("d3", "z", "d2"),
    ("far", "beyond", "edge"),
    ("actc", "c", "act"),
    ("farc", "beyond c", "edge"),
)

POS = 16
C_SWAP = [(i, i ^ 1) for i in range(POS)]
Y_SWAP = [(i, i ^ 2) for i in range(POS)]
CY_SWAP = [(i, i ^ 3) for i in range(POS)]
Z_RING = [(i, (i + 4) % POS) for i in range(POS)]
BEYOND = [(i, i + 1 if i % 2 else i - 1) for i in range(1, POS - 1)]
BEYOND_C = [(i, j ^ 1) for i, j in BEYOND]
X_SWAP = [(0, 1), (1, 0)]


def over_pos(pairs):
    return lambda v: lax.ppermute(v, "pos", pairs)


c_swap, y_swap, cy_swap = over_pos(C_SWAP), over_pos(Y_SWAP), over_pos(CY_SWAP)
z_ring = over_pos(Z_RING)


def x_swap(v):
    return lax.ppermute(v, "group", X_SWAP)


def project_kernel(idx, acts_hbm, gain, wq_hbm, wk_hbm, wv_hbm, *refs):
    outs, (acts, wq, wk, wv, sems) = refs[:4], refs[4:]
    copies = [
        pltpu.make_async_copy(src, dst, sems.at[n])
        for n, (src, dst) in enumerate(
            ((acts_hbm, acts), (wq_hbm, wq), (wk_hbm, wk), (wv_hbm, wv))
        )
    ]
    for copy in copies:
        copy.start()
    copies.pop(0).wait()
    a = acts[...].astype(F32)
    centre = a - jnp.mean(a, axis=-1, keepdims=True)
    normed = (
        centre * lax.rsqrt(jnp.mean(centre * centre, axis=-1, keepdims=True) + 1e-05) * gain[...]
    ).astype(BF16)
    for copy in copies:
        copy.wait()
    q = (jnp.dot(normed, wq[...], preferred_element_type=F32) * HK ** (-0.5))
    k = jnp.dot(normed, wk[...], preferred_element_type=F32)
    v = jnp.dot(normed, wv[...], preferred_element_type=F32)
    zeros = jnp.zeros((a.shape[0], HK), F32)
    packs = []
    for h in range(HEADS):
        packs.append(
            jnp.concatenate(
                [
                    v[:, HV * h : HV * (h + 1)],
                    k[:, HK * h : HK * (h + 1)],
                    zeros,
                    q[:, HK * h : HK * (h + 1)],
                ],
                axis=1,
            ).astype(BF16)
        )
    mine = 2 * idx[1] + idx[3]
    for h in range(HEADS):
        for s in range(HEADS):

            @pl.when((mine ^ s) == h)
            def _():
                outs[s][...] = packs[h]


def project(idx, acts, gain, wq, wk, wv):
    rows = acts.shape[0]
    return pl.pallas_call(
        project_kernel,
        out_shape=[jax.ShapeDtypeStruct((rows, 384), BF16)] * HEADS,
        in_specs=[SMEM, HBM, VMEM] + [HBM] * 3,
        out_specs=[VMEM] * HEADS,
        scratch_shapes=[
            pltpu.VMEM((128, 1536), BF16),
            pltpu.VMEM((1536, 256), BF16),
            pltpu.VMEM((1536, 256), BF16),
            pltpu.VMEM((1536, 768), BF16),
            pltpu.SemaphoreType.DMA((4,)),
        ],
        compiler_params=LIMIT,
        name="project",
    )(idx, acts, gain, wq, wk, wv)


def attend_kernel(*refs):
    packs, kvs, outs = refs[:4], refs[4:8], refs[8:]
    for s in range(2):
        rows = pl.ds(64 * s, 64)
        query = jnp.concatenate([p[rows, 256:384] for p in packs], axis=0)
        query = jnp.concatenate([jnp.zeros_like(query), query], axis=1)
        kv = jnp.concatenate([r[pl.ds(256 * s, 256), :] for r in kvs], axis=0)
        scores = lax.dot_general(
            query, kv, (((1,), (1,)), ((), ())), preferred_element_type=F32
        )
        weights = jnp.exp(scores - jnp.max(scores, axis=-1, keepdims=True))
        total = jnp.sum(weights, axis=-1, keepdims=True)
        mixed = (
            jnp.dot(weights.astype(BF16), kv, preferred_element_type=F32) / total
        ).astype(BF16)
        for j in range(4):
            outs[j][rows, :] = mixed[64 * j : 64 * (j + 1), :]


def attend(packs, kvs):
    return pl.pallas_call(
        attend_kernel,
        out_shape=[jax.ShapeDtypeStruct((128, 256), BF16)] * 4,
        in_specs=[VMEM] * 8,
        out_specs=[VMEM] * 4,
        compiler_params=LIMIT,
        name="attend",
    )(*packs, *kvs)


def output_kernel(idx, acts, wo, *refs):
    mixed, out = refs[:4], refs[4]
    mine = 2 * idx[1] + idx[3]
    total = acts[...].astype(F32)
    summed = None
    for s in range(4):
        rows = pl.ds(pl.multiple_of((mine ^ s) * HV, HV), HV)
        term = jnp.dot(mixed[s][:, :HV], wo[rows, :], preferred_element_type=F32)
        summed = term if summed is None else summed + term
    attended = (total + summed).astype(BF16).astype(F32)
    out[...] = jax.nn.gelu(attended).astype(BF16)


def output(idx, acts, wo, mixed):
    return pl.pallas_call(
        output_kernel,
        out_shape=jax.ShapeDtypeStruct(acts.shape, BF16),
        in_specs=[SMEM] + [VMEM] * 6,
        out_specs=VMEM,
        compiler_params=LIMIT,
        name="output",
    )(idx, acts, wo, *mixed)


def quarter(x):
    return pl.ds(pl.multiple_of(x * 384, 384), 384)


def rows_of(p, height):
    return pl.ds(pl.multiple_of(p * height, height), height)


A_ROWS = 352


def place(ref, zz, yy, c, col, wl, ws, wp):
    for n, cc in ((0, c), (1, 1 - c)):
        p = 4 * zz + 2 * yy + cc
        base = 176 * n
        wl[rows_of(p, 96), col] = ref[base : base + 96, :]
        ws[rows_of(p, 80), col] = ref[base + 96 : base + 176, :]
        base = A_ROWS + 96 * n
        wp[rows_of(p, 96), col] = ref[base : base + 96, :]


def early_kernel(idx, skip_own, skip_oth, *refs):
    pieces, (wl, ws, wp, part, late), (skip,) = refs[:12], refs[12:17], refs[17:]
    x, y, z, c = idx[0], idx[1], idx[2], idx[3]
    last = lax.rem(z + 1, 4)
    ws[rows_of(last, 320), :] = jnp.zeros((320, 768), BF16)
    keep, got, b0, d0 = pieces[:4]
    for ref, cc in ((keep, c), (got, 1 - c)):
        p = 4 * z + 2 * y + cc
        wl[rows_of(p, 96), :] = ref[:96, :]
        ws[rows_of(p, 80), :] = ref[96:176, :]
        wp[rows_of(p, 96), :] = ref[176:, :]
    place(b0, z, 1 - y, c, quarter(x), wl, ws, wp)
    place(d0, z, 1 - y, c, quarter(1 - x), wl, ws, wp)
    for k in (1, 2):
        place_plane(pieces[4 * k : 4 * k + 4], lax.rem(z + 4 - k, 4), x, y, c, wl, ws, wp)
    for s in range(2):
        for src, cc in ((skip_own, c), (skip_oth, 1 - c)):
            skip[pl.ds(pl.multiple_of(256 * s + 128 * cc, 128), 128), :] = src[
                pl.ds(128 * s, 128), :
            ]
    for zz in range(4):

        @pl.when(last == zz)
        def _():
            late[...] = skip[:, 320 * zz : 320 * (zz + 1)]

    part[...] = jnp.dot(skip[...], ws[...], preferred_element_type=F32)


def place_plane(pieces, zz, x, y, c, wl, ws, wp):
    a, b, xa, xb = pieces
    place(a, zz, y, c, quarter(x), wl, ws, wp)
    place(b, zz, 1 - y, c, quarter(x), wl, ws, wp)
    place(xa, zz, y, c, quarter(1 - x), wl, ws, wp)
    place(xb, zz, 1 - y, c, quarter(1 - x), wl, ws, wp)


WEIGHTS = [
    jax.ShapeDtypeStruct((1536, 768), BF16),
    jax.ShapeDtypeStruct((1280, 768), BF16),
    jax.ShapeDtypeStruct((1536, 768), BF16),
]


def early(idx, skip_own, skip_oth, pieces):
    return pl.pallas_call(
        early_kernel,
        out_shape=WEIGHTS
        + [jax.ShapeDtypeStruct((512, 768), F32), jax.ShapeDtypeStruct((512, 320), BF16)],
        in_specs=[SMEM] + [VMEM] * (2 + len(pieces)),
        out_specs=[VMEM] * 5,
        scratch_shapes=[pltpu.VMEM((512, 1280), BF16)],
        compiler_params=LIMIT,
        name="early",
    )(idx, skip_own, skip_oth, *pieces)


def merge_kernel(idx, act_own, act_oth, wl_in, ws_in, wp_in, part, late, *refs):
    del wl_in, ws_in, wp_in
    pieces, (merged, wl, ws, wp), (act,) = refs[:4], refs[4:8], refs[8:]
    x, y, z, c = idx[0], idx[1], idx[2], idx[3]
    last = lax.rem(z + 1, 4)
    place_plane(pieces, last, x, y, c, wl, ws, wp)
    for s in range(2):
        for src, cc in ((act_own, c), (act_oth, 1 - c)):
            act[pl.ds(pl.multiple_of(128 * s + 64 * cc, 64), 64), :] = src[
                pl.ds(64 * s, 64), :
            ]
    twice = (
        lax.broadcasted_iota(jnp.int32, (256, 128), 0) // 2
        == lax.broadcasted_iota(jnp.int32, (256, 128), 1)
    ).astype(BF16)
    lifted = jnp.dot(act[...], wl[...], preferred_element_type=F32).astype(BF16)
    terms = part[...] + jnp.dot(
        late[...], ws[rows_of(last, 320), :], preferred_element_type=F32
    )
    for s in range(2):
        raised = jnp.dot(twice, lifted[128 * s : 128 * (s + 1)], preferred_element_type=F32)
        merged[s, :, :] = (raised + terms[256 * s : 256 * (s + 1)]).astype(BF16)


def merge(idx, act_own, act_oth, weights, part, late, pieces):
    return pl.pallas_call(
        merge_kernel,
        out_shape=[jax.ShapeDtypeStruct((2, 256, 768), BF16)] + WEIGHTS,
        in_specs=[SMEM] + [VMEM] * (7 + len(pieces)),
        out_specs=[VMEM] * 4,
        scratch_shapes=[pltpu.VMEM((256, 1536), BF16)],
        input_output_aliases={3: 1, 4: 2, 5: 3},
        compiler_params=LIMIT,
        name="merge",
    )(idx, act_own, act_oth, *weights, part, late, *pieces)


def point_kernel(idx, depth, merged, wl, ws, wp, far, far_oth, oth, rest, spread):
    c = idx[3]
    ends = jnp.where(
        c == 0,
        jnp.concatenate([far[...], far_oth[...]], axis=0),
        jnp.concatenate([far_oth[...], far[...]], axis=0),
    )
    lifted = jnp.dot(ends[:, :1536], wl[...], preferred_element_type=F32).astype(BF16)
    ends = lifted.astype(F32) + jnp.dot(ends[:, 1536:], ws[...], preferred_element_type=F32)
    ends = ends.astype(BF16).astype(F32)
    taps = depth[:, pl.ds(pl.multiple_of(c * 768, 768), 768)]
    row = lax.broadcasted_iota(jnp.int32, (256, 768), 0)
    for s in range(2):
        here = merged[s, :, :].astype(F32)
        up = jnp.where(row == 0, ends[s : s + 1, :], pltpu.roll(here, 1, 0))
        down = jnp.where(row == 255, ends[s + 16 : s + 17, :], pltpu.roll(here, 255, 0))
        spread[pl.ds(256 * s, 256), :] = (
            taps[0:1] * up + taps[1:2] * here + taps[2:3] * down
        ).astype(BF16)
    for s in range(2):
        rest[pl.ds(128 * s, 128), :] = spread[
            pl.ds(pl.multiple_of(256 * s + 128 * c, 128), 128), :
        ]
    part = jnp.concatenate(
        [
            spread[pl.ds(pl.multiple_of(256 * s + 128 * (1 - c), 128), 128), :]
            for s in range(2)
        ],
        axis=0,
    )
    oth[...] = across(part, wp[...]).astype(BF16).reshape(oth.shape)


def across(rows, w):
    return lax.dot_general(rows, w, (((1,), (1,)), ((), ())), preferred_element_type=F32)


def point(idx, depth, merged, weights, far, far_oth):
    return pl.pallas_call(
        point_kernel,
        out_shape=[
            jax.ShapeDtypeStruct((2, 128, 1536), BF16),
            jax.ShapeDtypeStruct((256, 768), BF16),
        ],
        in_specs=[SMEM] + [VMEM] * 7,
        out_specs=[VMEM] * 2,
        scratch_shapes=[pltpu.VMEM((512, 768), BF16)],
        compiler_params=LIMIT,
        name="point",
    )(idx, depth, merged, *weights, far, far_oth)


def rest_kernel(rest, wp, own):
    own[...] = across(rest[...], wp[...]).reshape(own.shape)


def point_rest(rest, wp):
    return pl.pallas_call(
        rest_kernel,
        out_shape=jax.ShapeDtypeStruct((2, 128, 1536), F32),
        in_specs=[VMEM] * 2,
        out_specs=VMEM,
        compiler_params=LIMIT,
        name="point_rest",
    )(rest, wp)


def behind(v, *tokens):
    return lax.optimization_barrier((v,) + tokens)[0]


class Plan:
    def __init__(self, width, makers):
        self.width, self.makers, self.made, self.done = width, makers, {}, []

    def __getitem__(self, name):
        if name not in self.made:
            self.made[name] = self.makers[name]()
        return self.made[name]

    def send(self, how, name):
        v = self[name]
        if len(self.done) >= self.width:
            late = self.done[: len(self.done) - self.width + 1]
            v = behind(v, *(late if CUMULATIVE else late[-1:]))
        got = how(v)
        if how is not c_swap:
            self.done.append(got)
        return got


def in_hbm(v):
    return pltpu.with_memory_space_constraint(v, pltpu.HBM)


def split_kernel(idx, wl, ws, wp, keep, send, sems):
    c = idx[3]
    copies = []
    for out, cc in ((send, 1 - c), (keep, c)):
        cols = pl.ds(pl.multiple_of(768 * cc, 768), 768)
        for src, lo, hi in ((wl, 0, 96), (ws, 96, 176), (wp, 176, 272)):
            copies.append(
                pltpu.make_async_copy(src.at[:, cols], out.at[lo:hi], sems.at[len(copies)])
            )
    for copy in copies:
        copy.start()
    for copy in copies:
        copy.wait()


def split(idx, wl, ws, wp):
    return pl.pallas_call(
        split_kernel,
        out_shape=[jax.ShapeDtypeStruct((272, 768), BF16)] * 2,
        in_specs=[SMEM] + [HBM] * 3,
        out_specs=[VMEM] * 2,
        scratch_shapes=[
            pltpu.SemaphoreType.DMA((6,)),
        ],
        compiler_params=LIMIT,
        name="split",
    )(idx, wl, ws, wp)


def take_kernel(idx, keep, got, out, *, other):
    x = idx[0]
    cols = quarter(1 - x if other else x)
    for n, ref in enumerate((keep, got)):
        out[176 * n : 176 * (n + 1), :] = ref[:176, cols]
        out[A_ROWS + 96 * n : A_ROWS + 96 * (n + 1), :] = ref[176:, cols]


def take(idx, keep, got, other):
    return pl.pallas_call(
        functools.partial(take_kernel, other=other),
        out_shape=jax.ShapeDtypeStruct((544, 384), BF16),
        in_specs=[SMEM] + [VMEM] * 2,
        out_specs=VMEM,
        compiler_params=LIMIT,
        name="take",
    )(idx, keep, got)


def give_kernel(idx, act, skip, out):
    c = idx[3]
    out[2:16, :] = jnp.zeros((14, 2816), BF16)
    for s in range(2):
        for src, height, cols in ((act, 64, slice(0, 1536)), (skip, 128, slice(1536, 2816))):
            low, high = height * s, height * (s + 1) - 1
            out[s : s + 1, cols] = jnp.where(
                c == 0, src[low : low + 1, :], src[high : high + 1, :]
            )


def give(idx, act, skip):
    return pl.pallas_call(
        give_kernel,
        out_shape=jax.ShapeDtypeStruct((16, 2816), BF16),
        in_specs=[SMEM, VMEM, VMEM],
        out_specs=VMEM,
        compiler_params=LIMIT,
        name="give",
    )(idx, act, skip)


def on_device(
    acts, skips, norm_gain, w_query, w_key, w_value, w_out, w_lift, w_skip, depth_kernel, w_point
):
    pos = lax.axis_index("pos")
    x, c, y, z = lax.axis_index("group"), pos % 2, pos // 2 % 2, pos // 4
    idx = jnp.stack([x, y, z, c]).astype(jnp.int32)
    flat = acts.reshape(128, 1536)
    keep, send = split(idx, *map(in_hbm, (w_lift, w_skip, w_point.T)))
    got = c_swap(send)
    u0 = take(idx, keep, got, False)

    def projected():
        return project(
            idx,
            in_hbm(behind(flat, u0)),
            norm_gain.reshape(1, -1),
            *map(in_hbm, (w_query, w_key, w_value)),
        )

    def joined():
        packs = [plan[n] for n in ("q0", "qc", "qy", "qcy")]
        return jnp.concatenate(
            [p[:, :256].reshape(2, 64, 256) for p in packs], axis=1
        ).reshape(512, 256)

    def attended():
        return attend(
            [plan[n] for n in ("q0", "qc", "qy", "qcy")],
            [plan[n] for n in ("k0", "k1", "k2", "k3")],
        )

    makers = {
        "u0": lambda: u0,
        "c0": lambda: take(idx, keep, got, True),
        "packs": projected,
        "k0": joined,
        "mixes": attended,
        "act": lambda: output(idx, flat, w_out, [plan[n] for n in ("m0", "mc", "my", "mcy")]),
        "skip": lambda: jax.nn.gelu(skips.astype(F32)).astype(BF16).reshape(256, 1280),
        "edge": lambda: give(idx, plan["act"], plan["skip"]),
    }
    for n, way in enumerate(("0", "c", "y", "cy")):
        makers["p" + way] = lambda n=n: plan["packs"][n]
        makers["o" + way] = lambda n=n: plan["mixes"][n]
    makers["q0"], makers["m0"] = makers["p0"], makers["o0"]
    swaps = {"c": c_swap, "y": y_swap, "cy": cy_swap, "x": x_swap, "z": z_ring}
    swaps["beyond"], swaps["beyond c"] = over_pos(BEYOND), over_pos(BEYOND_C)

    def sender(how, src):
        return lambda: plan.send(swaps[how], src)

    for name, how, src in SENDS:
        makers[name] = sender(how, src)
    plan = Plan(WIDTH, makers)
    for name, _, _ in SENDS:
        plan[name]
    pieces = [keep, got, plan["b0"], plan["d0"]] + [
        plan[part + str(k)] for k in (1, 2) for part in "ubcd"
    ]
    *weights, part, late = early(idx, plan["skip"], plan["skipc"], pieces)
    merged, *weights = merge(
        idx, plan["act"], plan["actc"], weights, part, late,
        [plan[part + "3"] for part in "ubcd"],
    )
    oth, rest = point(idx, depth_kernel, merged, weights, plan["far"], plan["farc"])
    got = c_swap(oth)
    return (point_rest(rest, weights[2]) + got.astype(F32)).astype(BF16)


def extended(cells, sides, width):
    for axis, dim in sides:
        count = lax.axis_size(axis)
        ends = count - 1
        head = lax.slice_in_dim(cells, 0, width, axis=dim)
        tail = lax.slice_in_dim(cells, cells.shape[dim] - width, cells.shape[dim], axis=dim)
        cells = jnp.concatenate(
            [
                lax.ppermute(tail, axis, [(i, (i + 1) % count) for i in range(ends)]),
                cells,
                lax.ppermute(head, axis, [((i + 1) % count, i) for i in range(ends)]),
            ],
            axis=dim,
        )
    return cells


def on_device_plain(
    acts, skips, norm_gain, w_query, w_key, w_value, w_out, w_lift, w_skip, depth_kernel, w_point
):
    lift_full, skip_full, point_full = (
        lax.all_gather(w_lift, "pos", axis=0, tiled=True),
        lax.all_gather(w_skip, "pos", axis=0, tiled=True),
        lax.all_gather(w_point, "pos", axis=1, tiled=True),
    )
    seq_count, bin_rows, width = acts.shape
    actsf = acts.astype(jnp.float32)
    centre = actsf - jnp.mean(actsf, axis=-1, keepdims=True)
    normed = (
        centre * lax.rsqrt(jnp.mean(centre * centre, axis=-1, keepdims=True) + 1e-05) * norm_gain
    ).astype(jnp.bfloat16)
    flat = normed.reshape(seq_count * bin_rows, width)
    queries = (
        (jnp.dot(flat, w_query, preferred_element_type=jnp.float32) * HK ** (-0.5))
        .astype(jnp.bfloat16)
        .reshape(seq_count, bin_rows, HEADS, HK)
    )
    keys_here = (
        jnp.dot(flat, w_key, preferred_element_type=jnp.float32)
        .astype(jnp.bfloat16)
        .reshape(seq_count, bin_rows, HEADS * HK)
    )
    values_here = (
        jnp.dot(flat, w_value, preferred_element_type=jnp.float32)
        .astype(jnp.bfloat16)
        .reshape(seq_count, bin_rows, HEADS * HV)
    )
    running = jnp.full((seq_count, HEADS, bin_rows), -1e30, jnp.float32)
    key_piece = lax.all_gather(keys_here, "pos", axis=1, tiled=True)
    value_piece = lax.all_gather(values_here, "pos", axis=1, tiled=True)
    count = key_piece.shape[1]
    keyed = key_piece.reshape(seq_count, count, HEADS, HK)
    valued = value_piece.reshape(seq_count, count, HEADS, HV)
    scores = jnp.einsum("sqhd,skhd->shqk", queries, keyed, preferred_element_type=jnp.float32)
    newest = jnp.maximum(running, jnp.max(scores, axis=-1))
    weights = jnp.exp(scores - newest[..., None])
    totals = jnp.sum(weights, axis=-1)
    summed = jnp.einsum(
        "shqk,skhv->shqv", weights.astype(jnp.bfloat16), valued, preferred_element_type=jnp.float32
    )
    running, totals, summed = (newest, totals, summed)
    mixed = (
        (summed / totals[..., None])
        .transpose(0, 2, 1, 3)
        .reshape(seq_count * bin_rows, HEADS * HV)
        .astype(jnp.bfloat16)
    )
    attended = (
        actsf.reshape(seq_count * bin_rows, width)
        + jnp.dot(mixed, w_out, preferred_element_type=jnp.float32)
    ).astype(jnp.bfloat16)
    activated = jax.nn.gelu(attended.astype(jnp.float32)).astype(jnp.bfloat16)
    lifted = jnp.dot(activated, lift_full, preferred_element_type=jnp.float32)
    lifted = lifted.astype(jnp.bfloat16).reshape(seq_count, bin_rows, width)
    raised = jnp.repeat(lifted, 2, axis=1).reshape(seq_count * 2 * bin_rows, width)
    skip_act = (
        jax.nn.gelu(skips.astype(jnp.float32))
        .astype(jnp.bfloat16)
        .reshape(seq_count * 2 * bin_rows, skips.shape[2])
    )
    skip_term = jnp.dot(skip_act, skip_full, preferred_element_type=jnp.float32)
    merged = (
        (raised.astype(jnp.float32) + skip_term)
        .astype(jnp.bfloat16)
        .reshape(seq_count, 2 * bin_rows, width)
    )
    padded = extended(merged, (("pos", 1),), 1)
    paddedf = padded.astype(jnp.float32)
    spread = (
        depth_kernel[0] * paddedf[:, :-2]
        + depth_kernel[1] * paddedf[:, 1:-1]
        + depth_kernel[2] * paddedf[:, 2:]
    ).astype(jnp.bfloat16)
    spread = spread.reshape(seq_count * 2 * bin_rows, width)
    decoded = jnp.dot(spread, point_full, preferred_element_type=jnp.float32)
    return decoded.astype(jnp.bfloat16).reshape(seq_count, 2 * bin_rows, width)


def solution(mesh):
    planned = dict(mesh.shape) == {"group": 2, "pos": POS}
    return jax.shard_map(
        on_device if planned else on_device_plain,
        mesh=mesh,
        in_specs=(
            P("group", "pos", None),
            P("group", "pos", None),
            P(),
            P(),
            P(),
            P(),
            P(),
            P("pos", None),
            P("pos", None),
            P(),
            P(None, "pos"),
        ),
        out_specs=P("group", "pos", None),
        check_vma=False,
    )
```

```python
import functools

import jax
import jax.numpy as jnp
from jax import lax
from jax.experimental import pallas as pl
from jax.experimental.pallas import tpu as pltpu
from jax.sharding import PartitionSpec as P

HEADS = 4
HK = 64
HV = 192
F32 = jnp.float32
BF16 = jnp.bfloat16
ANY = pl.BlockSpec(memory_space=pl.ANY)
VMEM = pl.BlockSpec(memory_space=pltpu.VMEM)
HBM = pl.BlockSpec(memory_space=pltpu.HBM)
SMEM = pl.BlockSpec(memory_space=pltpu.SMEM)
LIMIT = pltpu.CompilerParams(vmem_limit_bytes=20 * 1024 * 1024)

WIDTH = 5
CUMULATIVE = True
FREE = ()
SENDS = (
    ("u1", "z", "u0"),
    ("b0", "y", "u0"),
    ("qy", "y", "py"),
    ("u2", "z", "u1"),
    ("c1", "x", "u1"),
    ("qcy", "cy", "pcy"),
    ("b1", "y", "u1"),
    ("k1", "z", "k0"),
    ("c2", "x", "u2"),
    ("b2", "y", "u2"),
    ("u3", "z", "u2"),
    ("qc", "c", "pc"),
    ("k2", "z", "k1"),
    ("skipc", "c", "skip"),
    ("d2", "y", "c2"),
    ("d0", "x", "b0"),
    ("k3", "z", "k2"),
    ("b3", "y", "u3"),
    ("d1", "x", "b1"),
    ("my", "y", "oy"),
    ("mc", "c", "oc"),
    ("mcy", "cy", "ocy"),
    ("c3", "x", "u3"),
    ("d3", "z", "d2"),
    ("far", "beyond", "edge"),
    ("actc", "c", "act"),
    ("farc", "beyond c", "edge"),
)

POS = 16
C_SWAP = [(i, i ^ 1) for i in range(POS)]
Y_SWAP = [(i, i ^ 2) for i in range(POS)]
CY_SWAP = [(i, i ^ 3) for i in range(POS)]
Z_RING = [(i, (i + 4) % POS) for i in range(POS)]
BEYOND = [(i, i + 1 if i % 2 else i - 1) for i in range(1, POS - 1)]
BEYOND_C = [(i, j ^ 1) for i, j in BEYOND]
X_SWAP = [(0, 1), (1, 0)]


def over_pos(pairs):
    return lambda v: lax.ppermute(v, "pos", pairs)


c_swap, y_swap, cy_swap = over_pos(C_SWAP), over_pos(Y_SWAP), over_pos(CY_SWAP)
z_ring = over_pos(Z_RING)


def x_swap(v):
    return lax.ppermute(v, "group", X_SWAP)


def project_kernel(idx, acts_hbm, gain, wq_hbm, wk_hbm, wv_hbm, *refs):
    outs, (acts, wq, wk, wv, sems) = refs[:4], refs[4:]
    copies = [
        pltpu.make_async_copy(src, dst, sems.at[n])
        for n, (src, dst) in enumerate(
            ((acts_hbm, acts), (wq_hbm, wq), (wk_hbm, wk), (wv_hbm, wv))
        )
    ]
    for copy in copies:
        copy.start()
    copies.pop(0).wait()
    a = acts[...].astype(F32)
    centre = a - jnp.mean(a, axis=-1, keepdims=True)
    normed = (
        centre * lax.rsqrt(jnp.mean(centre * centre, axis=-1, keepdims=True) + 1e-05) * gain[...]
    ).astype(BF16)
    for copy in copies:
        copy.wait()
    q = (jnp.dot(normed, wq[...], preferred_element_type=F32) * HK ** (-0.5))
    k = jnp.dot(normed, wk[...], preferred_element_type=F32)
    v = jnp.dot(normed, wv[...], preferred_element_type=F32)
    zeros = jnp.zeros((a.shape[0], HK), F32)
    packs = []
    for h in range(HEADS):
        packs.append(
            jnp.concatenate(
                [
                    v[:, HV * h : HV * (h + 1)],
                    k[:, HK * h : HK * (h + 1)],
                    zeros,
                    q[:, HK * h : HK * (h + 1)],
                ],
                axis=1,
            ).astype(BF16)
        )
    mine = 2 * idx[1] + idx[3]
    for h in range(HEADS):
        for s in range(HEADS):

            @pl.when((mine ^ s) == h)
            def _():
                outs[s][...] = packs[h]


def project(idx, acts, gain, wq, wk, wv):
    rows = acts.shape[0]
    return pl.pallas_call(
        project_kernel,
        out_shape=[jax.ShapeDtypeStruct((rows, 384), BF16)] * HEADS,
        in_specs=[SMEM, HBM, VMEM] + [HBM] * 3,
        out_specs=[VMEM] * HEADS,
        scratch_shapes=[
            pltpu.VMEM((128, 1536), BF16),
            pltpu.VMEM((1536, 256), BF16),
            pltpu.VMEM((1536, 256), BF16),
            pltpu.VMEM((1536, 768), BF16),
            pltpu.SemaphoreType.DMA((4,)),
        ],
        compiler_params=LIMIT,
        name="project",
    )(idx, acts, gain, wq, wk, wv)


def attend_kernel(*refs):
    packs, kvs, outs = refs[:4], refs[4:8], refs[8:]
    for s in range(2):
        rows = pl.ds(64 * s, 64)
        query = jnp.concatenate([p[rows, 256:384] for p in packs], axis=0)
        query = jnp.concatenate([jnp.zeros_like(query), query], axis=1)
        kv = jnp.concatenate([r[pl.ds(256 * s, 256), :] for r in kvs], axis=0)
        scores = lax.dot_general(
            query, kv, (((1,), (1,)), ((), ())), preferred_element_type=F32
        )
        weights = jnp.exp(scores - jnp.max(scores, axis=-1, keepdims=True))
        total = jnp.sum(weights, axis=-1, keepdims=True)
        mixed = (
            jnp.dot(weights.astype(BF16), kv, preferred_element_type=F32) / total
        ).astype(BF16)
        for j in range(4):
            outs[j][rows, :] = mixed[64 * j : 64 * (j + 1), :]


def attend(packs, kvs):
    return pl.pallas_call(
        attend_kernel,
        out_shape=[jax.ShapeDtypeStruct((128, 256), BF16)] * 4,
        in_specs=[VMEM] * 8,
        out_specs=[VMEM] * 4,
        compiler_params=LIMIT,
        name="attend",
    )(*packs, *kvs)


def output_kernel(idx, acts, wo, *refs):
    mixed, out = refs[:4], refs[4]
    mine = 2 * idx[1] + idx[3]
    total = acts[...].astype(F32)
    summed = None
    for s in range(4):
        rows = pl.ds(pl.multiple_of((mine ^ s) * HV, HV), HV)
        term = jnp.dot(mixed[s][:, :HV], wo[rows, :], preferred_element_type=F32)
        summed = term if summed is None else summed + term
    attended = (total + summed).astype(BF16).astype(F32)
    out[...] = jax.nn.gelu(attended).astype(BF16)


def output(idx, acts, wo, mixed):
    return pl.pallas_call(
        output_kernel,
        out_shape=jax.ShapeDtypeStruct(acts.shape, BF16),
        in_specs=[SMEM] + [VMEM] * 6,
        out_specs=VMEM,
        compiler_params=LIMIT,
        name="output",
    )(idx, acts, wo, *mixed)


def quarter(x):
    return pl.ds(pl.multiple_of(x * 384, 384), 384)


def rows_of(p, height):
    return pl.ds(pl.multiple_of(p * height, height), height)


A_ROWS = 352


def place(ref, zz, yy, c, col, wl, ws, wp):
    for n, cc in ((0, c), (1, 1 - c)):
        p = 4 * zz + 2 * yy + cc
        base = 176 * n
        wl[rows_of(p, 96), col] = ref[base : base + 96, :]
        ws[rows_of(p, 80), col] = ref[base + 96 : base + 176, :]
        base = A_ROWS + 96 * n
        wp[rows_of(p, 96), col] = ref[base : base + 96, :]


def early_kernel(idx, skip_own, skip_oth, *refs):
    pieces, (wl, ws, wp, part, late), (skip,) = refs[:12], refs[12:17], refs[17:]
    x, y, z, c = idx[0], idx[1], idx[2], idx[3]
    last = lax.rem(z + 1, 4)
    ws[rows_of(last, 320), :] = jnp.zeros((320, 768), BF16)
    keep, got, b0, d0 = pieces[:4]
    for ref, cc in ((keep, c), (got, 1 - c)):
        p = 4 * z + 2 * y + cc
        wl[rows_of(p, 96), :] = ref[:96, :]
        ws[rows_of(p, 80), :] = ref[96:176, :]
        wp[rows_of(p, 96), :] = ref[176:, :]
    place(b0, z, 1 - y, c, quarter(x), wl, ws, wp)
    place(d0, z, 1 - y, c, quarter(1 - x), wl, ws, wp)
    for k in (1, 2):
        place_plane(pieces[4 * k : 4 * k + 4], lax.rem(z + 4 - k, 4), x, y, c, wl, ws, wp)
    for s in range(2):
        for src, cc in ((skip_own, c), (skip_oth, 1 - c)):
            skip[pl.ds(pl.multiple_of(256 * s + 128 * cc, 128), 128), :] = src[
                pl.ds(128 * s, 128), :
            ]
    for zz in range(4):

        @pl.when(last == zz)
        def _():
            late[...] = skip[:, 320 * zz : 320 * (zz + 1)]

    part[...] = jnp.dot(skip[...], ws[...], preferred_element_type=F32)


def place_plane(pieces, zz, x, y, c, wl, ws, wp):
    a, b, xa, xb = pieces
    place(a, zz, y, c, quarter(x), wl, ws, wp)
    place(b, zz, 1 - y, c, quarter(x), wl, ws, wp)
    place(xa, zz, y, c, quarter(1 - x), wl, ws, wp)
    place(xb, zz, 1 - y, c, quarter(1 - x), wl, ws, wp)


WEIGHTS = [
    jax.ShapeDtypeStruct((1536, 768), BF16),
    jax.ShapeDtypeStruct((1280, 768), BF16),
    jax.ShapeDtypeStruct((1536, 768), BF16),
]


def ordered(c, own, other):
    return jnp.where(
        c == 0, jnp.concatenate([own, other], axis=0), jnp.concatenate([other, own], axis=0)
    )


def early(idx, skip_own, skip_oth, pieces):
    return pl.pallas_call(
        early_kernel,
        out_shape=WEIGHTS
        + [jax.ShapeDtypeStruct((512, 768), F32), jax.ShapeDtypeStruct((512, 320), BF16)],
        in_specs=[SMEM] + [VMEM] * (2 + len(pieces)),
        out_specs=[VMEM] * 5,
        scratch_shapes=[pltpu.VMEM((512, 1280), BF16)],
        compiler_params=LIMIT,
        name="early",
    )(idx, skip_own, skip_oth, *pieces)


def decode_kernel(idx, depth, act_own, act_oth, far, far_oth, wl_in, ws_in, wp_in, part, late, *refs):
    del wl_in, ws_in, wp_in
    pieces, (oth, rest, wl, ws, wp), (act, spread) = refs[:4], refs[4:9], refs[9:]
    x, y, z, c = idx[0], idx[1], idx[2], idx[3]
    last = lax.rem(z + 1, 4)
    place_plane(pieces, last, x, y, c, wl, ws, wp)
    for s in range(2):
        for src, cc in ((act_own, c), (act_oth, 1 - c)):
            act[pl.ds(pl.multiple_of(128 * s + 64 * cc, 64), 64), :] = src[
                pl.ds(64 * s, 64), :
            ]
    beyond = ordered(c, far[...], far_oth[...])
    act[256:288, :] = beyond[:, :1536]
    twice = (
        lax.broadcasted_iota(jnp.int32, (256, 128), 0) // 2
        == lax.broadcasted_iota(jnp.int32, (256, 128), 1)
    ).astype(BF16)
    lifted = jnp.dot(act[...], wl[...], preferred_element_type=F32).astype(BF16)
    terms = part[...] + jnp.dot(
        late[...], ws[rows_of(last, 320), :], preferred_element_type=F32
    )
    ends = lifted[256:].astype(F32) + jnp.dot(
        beyond[:, 1536:], ws[...], preferred_element_type=F32
    )
    ends = ends.astype(BF16).astype(F32)
    taps = depth[:, pl.ds(pl.multiple_of(c * 768, 768), 768)]
    row = lax.broadcasted_iota(jnp.int32, (256, 768), 0)
    for s in range(2):
        raised = jnp.dot(twice, lifted[128 * s : 128 * (s + 1)], preferred_element_type=F32)
        here = (raised + terms[256 * s : 256 * (s + 1)]).astype(BF16).astype(F32)
        up = jnp.where(row == 0, ends[s : s + 1, :], pltpu.roll(here, 1, 0))
        down = jnp.where(row == 255, ends[s + 16 : s + 17, :], pltpu.roll(here, 255, 0))
        spread[pl.ds(256 * s, 256), :] = (
            taps[0:1] * up + taps[1:2] * here + taps[2:3] * down
        ).astype(BF16)
    for s in range(2):
        rest[pl.ds(128 * s, 128), :] = spread[
            pl.ds(pl.multiple_of(256 * s + 128 * c, 128), 128), :
        ]
    rows = jnp.concatenate(
        [
            spread[pl.ds(pl.multiple_of(256 * s + 128 * (1 - c), 128), 128), :]
            for s in range(2)
        ],
        axis=0,
    )
    oth[...] = across(rows, wp[...]).astype(BF16).reshape(oth.shape)


def decode(idx, depth, act_own, act_oth, far, far_oth, weights, part, late, pieces):
    return pl.pallas_call(
        decode_kernel,
        out_shape=[
            jax.ShapeDtypeStruct((2, 128, 1536), BF16),
            jax.ShapeDtypeStruct((256, 768), BF16),
        ]
        + WEIGHTS,
        in_specs=[SMEM] + [VMEM] * (10 + len(pieces)),
        out_specs=[VMEM] * 5,
        scratch_shapes=[pltpu.VMEM((288, 1536), BF16), pltpu.VMEM((512, 768), BF16)],
        input_output_aliases={6: 2, 7: 3, 8: 4},
        compiler_params=LIMIT,
        name="decode",
    )(idx, depth, act_own, act_oth, far, far_oth, *weights, part, late, *pieces)


def across(rows, w):
    return lax.dot_general(rows, w, (((1,), (1,)), ((), ())), preferred_element_type=F32)


def rest_kernel(rest, wp, own):
    own[...] = across(rest[...], wp[...]).reshape(own.shape)


def point_rest(rest, wp):
    return pl.pallas_call(
        rest_kernel,
        out_shape=jax.ShapeDtypeStruct((2, 128, 1536), F32),
        in_specs=[VMEM] * 2,
        out_specs=VMEM,
        compiler_params=LIMIT,
        name="point_rest",
    )(rest, wp)


def behind(v, *tokens):
    return lax.optimization_barrier((v,) + tokens)[0]


class Plan:
    def __init__(self, width, makers):
        self.width, self.makers, self.made, self.done = width, makers, {}, []

    def __getitem__(self, name):
        if name not in self.made:
            self.made[name] = self.makers[name]()
        return self.made[name]

    def send(self, how, name, free):
        v = self[name]
        if not free and len(self.done) >= self.width:
            late = self.done[: len(self.done) - self.width + 1]
            v = behind(v, *(late if CUMULATIVE else late[-1:]))
        got = how(v)
        if not free and how is not c_swap:
            self.done.append(got)
        return got


def in_hbm(v):
    return pltpu.with_memory_space_constraint(v, pltpu.HBM)


def split_kernel(idx, wl, ws, wp, keep, send, sems):
    c = idx[3]
    copies = []
    for out, cc in ((send, 1 - c), (keep, c)):
        cols = pl.ds(pl.multiple_of(768 * cc, 768), 768)
        for src, lo, hi in ((wl, 0, 96), (ws, 96, 176), (wp, 176, 272)):
            copies.append(
                pltpu.make_async_copy(src.at[:, cols], out.at[lo:hi], sems.at[len(copies)])
            )
    for copy in copies:
        copy.start()
    for copy in copies:
        copy.wait()


def split(idx, wl, ws, wp):
    return pl.pallas_call(
        split_kernel,
        out_shape=[jax.ShapeDtypeStruct((272, 768), BF16)] * 2,
        in_specs=[SMEM] + [HBM] * 3,
        out_specs=[VMEM] * 2,
        scratch_shapes=[
            pltpu.SemaphoreType.DMA((6,)),
        ],
        compiler_params=LIMIT,
        name="split",
    )(idx, wl, ws, wp)


def take_kernel(idx, keep, got, out, *, other):
    x = idx[0]
    cols = quarter(1 - x if other else x)
    for n, ref in enumerate((keep, got)):
        out[176 * n : 176 * (n + 1), :] = ref[:176, cols]
        out[A_ROWS + 96 * n : A_ROWS + 96 * (n + 1), :] = ref[176:, cols]


def take(idx, keep, got, other):
    return pl.pallas_call(
        functools.partial(take_kernel, other=other),
        out_shape=jax.ShapeDtypeStruct((544, 384), BF16),
        in_specs=[SMEM] + [VMEM] * 2,
        out_specs=VMEM,
        compiler_params=LIMIT,
        name="take",
    )(idx, keep, got)


def give_kernel(idx, act, skip, out):
    c = idx[3]
    out[2:16, :] = jnp.zeros((14, 2816), BF16)
    for s in range(2):
        for src, height, cols in ((act, 64, slice(0, 1536)), (skip, 128, slice(1536, 2816))):
            low, high = height * s, height * (s + 1) - 1
            out[s : s + 1, cols] = jnp.where(
                c == 0, src[low : low + 1, :], src[high : high + 1, :]
            )


def give(idx, act, skip):
    return pl.pallas_call(
        give_kernel,
        out_shape=jax.ShapeDtypeStruct((16, 2816), BF16),
        in_specs=[SMEM, VMEM, VMEM],
        out_specs=VMEM,
        compiler_params=LIMIT,
        name="give",
    )(idx, act, skip)


def on_device(
    acts, skips, norm_gain, w_query, w_key, w_value, w_out, w_lift, w_skip, depth_kernel, w_point
):
    pos = lax.axis_index("pos")
    x, c, y, z = lax.axis_index("group"), pos % 2, pos // 2 % 2, pos // 4
    idx = jnp.stack([x, y, z, c]).astype(jnp.int32)
    flat = acts.reshape(128, 1536)
    keep, send = split(idx, *map(in_hbm, (w_lift, w_skip, w_point.T)))
    got = c_swap(send)
    u0 = take(idx, keep, got, False)

    def projected():
        return project(
            idx,
            in_hbm(behind(flat, u0)),
            norm_gain.reshape(1, -1),
            *map(in_hbm, (w_query, w_key, w_value)),
        )

    def joined():
        packs = [plan[n] for n in ("q0", "qc", "qy", "qcy")]
        return jnp.concatenate(
            [p[:, :256].reshape(2, 64, 256) for p in packs], axis=1
        ).reshape(512, 256)

    def attended():
        return attend(
            [plan[n] for n in ("q0", "qc", "qy", "qcy")],
            [plan[n] for n in ("k0", "k1", "k2", "k3")],
        )

    makers = {
        "u0": lambda: u0,
        "c0": lambda: take(idx, keep, got, True),
        "packs": projected,
        "k0": joined,
        "mixes": attended,
        "act": lambda: output(idx, flat, w_out, [plan[n] for n in ("m0", "mc", "my", "mcy")]),
        "skip": lambda: jax.nn.gelu(skips.astype(F32)).astype(BF16).reshape(256, 1280),
        "edge": lambda: give(idx, plan["act"], plan["skip"]),
    }
    for n, way in enumerate(("0", "c", "y", "cy")):
        makers["p" + way] = lambda n=n: plan["packs"][n]
        makers["o" + way] = lambda n=n: plan["mixes"][n]
    makers["q0"], makers["m0"] = makers["p0"], makers["o0"]
    swaps = {"c": c_swap, "y": y_swap, "cy": cy_swap, "x": x_swap, "z": z_ring}
    swaps["beyond"], swaps["beyond c"] = over_pos(BEYOND), over_pos(BEYOND_C)

    def sender(name, how, src):
        return lambda: plan.send(swaps[how], src, name in FREE)

    for name, how, src in SENDS:
        makers[name] = sender(name, how, src)
    plan = Plan(WIDTH, makers)
    for name, _, _ in SENDS:
        plan[name]
    pieces = [keep, got, plan["b0"], plan["d0"]] + [
        plan[kind + str(k)] for k in (1, 2) for kind in "ubcd"
    ]
    *weights, part, late = early(idx, plan["skip"], plan["skipc"], pieces)
    oth, rest, *weights = decode(
        idx, depth_kernel, *(plan[n] for n in ("act", "actc", "far", "farc")), weights, part, late,
        [plan[kind + "3"] for kind in "ubcd"],
    )
    got = c_swap(oth)
    return (point_rest(rest, weights[2]) + got.astype(F32)).astype(BF16)


def extended(cells, sides, width):
    for axis, dim in sides:
        count = lax.axis_size(axis)
        ends = count - 1
        head = lax.slice_in_dim(cells, 0, width, axis=dim)
        tail = lax.slice_in_dim(cells, cells.shape[dim] - width, cells.shape[dim], axis=dim)
        cells = jnp.concatenate(
            [
                lax.ppermute(tail, axis, [(i, (i + 1) % count) for i in range(ends)]),
                cells,
                lax.ppermute(head, axis, [((i + 1) % count, i) for i in range(ends)]),
            ],
            axis=dim,
        )
    return cells


def on_device_plain(
    acts, skips, norm_gain, w_query, w_key, w_value, w_out, w_lift, w_skip, depth_kernel, w_point
):
    lift_full, skip_full, point_full = (
        lax.all_gather(w_lift, "pos", axis=0, tiled=True),
        lax.all_gather(w_skip, "pos", axis=0, tiled=True),
        lax.all_gather(w_point, "pos", axis=1, tiled=True),
    )
    seq_count, bin_rows, width = acts.shape
    actsf = acts.astype(jnp.float32)
    centre = actsf - jnp.mean(actsf, axis=-1, keepdims=True)
    normed = (
        centre * lax.rsqrt(jnp.mean(centre * centre, axis=-1, keepdims=True) + 1e-05) * norm_gain
    ).astype(jnp.bfloat16)
    flat = normed.reshape(seq_count * bin_rows, width)
    queries = (
        (jnp.dot(flat, w_query, preferred_element_type=jnp.float32) * HK ** (-0.5))
        .astype(jnp.bfloat16)
        .reshape(seq_count, bin_rows, HEADS, HK)
    )
    keys_here = (
        jnp.dot(flat, w_key, preferred_element_type=jnp.float32)
        .astype(jnp.bfloat16)
        .reshape(seq_count, bin_rows, HEADS * HK)
    )
    values_here = (
        jnp.dot(flat, w_value, preferred_element_type=jnp.float32)
        .astype(jnp.bfloat16)
        .reshape(seq_count, bin_rows, HEADS * HV)
    )
    running = jnp.full((seq_count, HEADS, bin_rows), -1e30, jnp.float32)
    key_piece = lax.all_gather(keys_here, "pos", axis=1, tiled=True)
    value_piece = lax.all_gather(values_here, "pos", axis=1, tiled=True)
    count = key_piece.shape[1]
    keyed = key_piece.reshape(seq_count, count, HEADS, HK)
    valued = value_piece.reshape(seq_count, count, HEADS, HV)
    scores = jnp.einsum("sqhd,skhd->shqk", queries, keyed, preferred_element_type=jnp.float32)
    newest = jnp.maximum(running, jnp.max(scores, axis=-1))
    weights = jnp.exp(scores - newest[..., None])
    totals = jnp.sum(weights, axis=-1)
    summed = jnp.einsum(
        "shqk,skhv->shqv", weights.astype(jnp.bfloat16), valued, preferred_element_type=jnp.float32
    )
    running, totals, summed = (newest, totals, summed)
    mixed = (
        (summed / totals[..., None])
        .transpose(0, 2, 1, 3)
        .reshape(seq_count * bin_rows, HEADS * HV)
        .astype(jnp.bfloat16)
    )
    attended = (
        actsf.reshape(seq_count * bin_rows, width)
        + jnp.dot(mixed, w_out, preferred_element_type=jnp.float32)
    ).astype(jnp.bfloat16)
    activated = jax.nn.gelu(attended.astype(jnp.float32)).astype(jnp.bfloat16)
    lifted = jnp.dot(activated, lift_full, preferred_element_type=jnp.float32)
    lifted = lifted.astype(jnp.bfloat16).reshape(seq_count, bin_rows, width)
    raised = jnp.repeat(lifted, 2, axis=1).reshape(seq_count * 2 * bin_rows, width)
    skip_act = (
        jax.nn.gelu(skips.astype(jnp.float32))
        .astype(jnp.bfloat16)
        .reshape(seq_count * 2 * bin_rows, skips.shape[2])
    )
    skip_term = jnp.dot(skip_act, skip_full, preferred_element_type=jnp.float32)
    merged = (
        (raised.astype(jnp.float32) + skip_term)
        .astype(jnp.bfloat16)
        .reshape(seq_count, 2 * bin_rows, width)
    )
    padded = extended(merged, (("pos", 1),), 1)
    paddedf = padded.astype(jnp.float32)
    spread = (
        depth_kernel[0] * paddedf[:, :-2]
        + depth_kernel[1] * paddedf[:, 1:-1]
        + depth_kernel[2] * paddedf[:, 2:]
    ).astype(jnp.bfloat16)
    spread = spread.reshape(seq_count * 2 * bin_rows, width)
    decoded = jnp.dot(spread, point_full, preferred_element_type=jnp.float32)
    return decoded.astype(jnp.bfloat16).reshape(seq_count, 2 * bin_rows, width)


def solution(mesh):
    planned = dict(mesh.shape) == {"group": 2, "pos": POS}
    return jax.shard_map(
        on_device if planned else on_device_plain,
        mesh=mesh,
        in_specs=(
            P("group", "pos", None),
            P("group", "pos", None),
            P(),
            P(),
            P(),
            P(),
            P(),
            P("pos", None),
            P("pos", None),
            P(),
            P(None, "pos"),
        ),
        out_specs=P("group", "pos", None),
        check_vma=False,
    )
```

```python
import functools

import jax
import jax.numpy as jnp
from jax import lax
from jax.experimental import pallas as pl
from jax.experimental.pallas import tpu as pltpu
from jax.sharding import PartitionSpec as P

HEADS = 4
HK = 64
HV = 192
F32 = jnp.float32
BF16 = jnp.bfloat16
ANY = pl.BlockSpec(memory_space=pl.ANY)
VMEM = pl.BlockSpec(memory_space=pltpu.VMEM)
HBM = pl.BlockSpec(memory_space=pltpu.HBM)
SMEM = pl.BlockSpec(memory_space=pltpu.SMEM)
LIMIT = pltpu.CompilerParams(vmem_limit_bytes=20 * 1024 * 1024)

WIDTH = 5
CUMULATIVE = True
FREE = ("far", "farc",)
SENDS = (
    ("u1", "z", "u0"),
    ("qy", "y", "py"),
    ("qcy", "cy", "pcy"),
    ("b0", "y", "u0"),
    ("u2", "z", "u1"),
    ("c1", "x", "u1"),
    ("b1", "y", "u1"),
    ("k1", "z", "k0"),
    ("c2", "x", "u2"),
    ("b2", "y", "u2"),
    ("u3", "z", "u2"),
    ("qc", "c", "pc"),
    ("k2", "z", "k1"),
    ("skipc", "c", "skip"),
    ("d2", "y", "c2"),
    ("d0", "x", "b0"),
    ("k3", "z", "k2"),
    ("b3", "y", "u3"),
    ("d1", "x", "b1"),
    ("d3", "z", "d2"),
    ("my", "y", "oy"),
    ("mc", "c", "oc"),
    ("c3", "x", "u3"),
    ("mcy", "cy", "ocy"),
    ("actc", "c", "act"),
    ("far", "beyond", "edge"),
    ("farc", "beyond c", "edge"),
)

POS = 16
C_SWAP = [(i, i ^ 1) for i in range(POS)]
Y_SWAP = [(i, i ^ 2) for i in range(POS)]
CY_SWAP = [(i, i ^ 3) for i in range(POS)]
Z_RING = [(i, (i + 4) % POS) for i in range(POS)]
BEYOND = [(i, i + 1 if i % 2 else i - 1) for i in range(1, POS - 1)]
BEYOND_C = [(i, j ^ 1) for i, j in BEYOND]
X_SWAP = [(0, 1), (1, 0)]


def over_pos(pairs):
    return lambda v: lax.ppermute(v, "pos", pairs)


c_swap, y_swap, cy_swap = over_pos(C_SWAP), over_pos(Y_SWAP), over_pos(CY_SWAP)
z_ring = over_pos(Z_RING)


def x_swap(v):
    return lax.ppermute(v, "group", X_SWAP)


def project_kernel(idx, acts_hbm, gain, wq_hbm, wk_hbm, wv_hbm, *refs):
    outs, (acts, wq, wk, wv, sems) = refs[:4], refs[4:]
    copies = [
        pltpu.make_async_copy(src, dst, sems.at[n])
        for n, (src, dst) in enumerate(
            ((acts_hbm, acts), (wq_hbm, wq), (wk_hbm, wk), (wv_hbm, wv))
        )
    ]
    for copy in copies:
        copy.start()
    copies.pop(0).wait()
    a = acts[...].astype(F32)
    centre = a - jnp.mean(a, axis=-1, keepdims=True)
    normed = (
        centre * lax.rsqrt(jnp.mean(centre * centre, axis=-1, keepdims=True) + 1e-05) * gain[...]
    ).astype(BF16)
    for copy in copies:
        copy.wait()
    q = (jnp.dot(normed, wq[...], preferred_element_type=F32) * HK ** (-0.5))
    k = jnp.dot(normed, wk[...], preferred_element_type=F32)
    v = jnp.dot(normed, wv[...], preferred_element_type=F32)
    zeros = jnp.zeros((a.shape[0], HK), F32)
    packs = []
    for h in range(HEADS):
        packs.append(
            jnp.concatenate(
                [
                    v[:, HV * h : HV * (h + 1)],
                    k[:, HK * h : HK * (h + 1)],
                    zeros,
                    q[:, HK * h : HK * (h + 1)],
                ],
                axis=1,
            ).astype(BF16)
        )
    mine = 2 * idx[1] + idx[3]
    for h in range(HEADS):
        for s in range(HEADS):

            @pl.when((mine ^ s) == h)
            def _():
                outs[s][...] = packs[h]


def project(idx, acts, gain, wq, wk, wv):
    rows = acts.shape[0]
    return pl.pallas_call(
        project_kernel,
        out_shape=[jax.ShapeDtypeStruct((rows, 384), BF16)] * HEADS,
        in_specs=[SMEM, HBM, VMEM] + [HBM] * 3,
        out_specs=[VMEM] * HEADS,
        scratch_shapes=[
            pltpu.VMEM((128, 1536), BF16),
            pltpu.VMEM((1536, 256), BF16),
            pltpu.VMEM((1536, 256), BF16),
            pltpu.VMEM((1536, 768), BF16),
            pltpu.SemaphoreType.DMA((4,)),
        ],
        compiler_params=LIMIT,
        name="project",
    )(idx, acts, gain, wq, wk, wv)


def attend_kernel(*refs):
    packs, kvs, outs = refs[:4], refs[4:8], refs[8:]
    for s in range(2):
        rows = pl.ds(64 * s, 64)
        query = jnp.concatenate([p[rows, 256:384] for p in packs], axis=0)
        query = jnp.concatenate([jnp.zeros_like(query), query], axis=1)
        kv = jnp.concatenate([r[pl.ds(256 * s, 256), :] for r in kvs], axis=0)
        scores = lax.dot_general(
            query, kv, (((1,), (1,)), ((), ())), preferred_element_type=F32
        )
        weights = jnp.exp(scores - jnp.max(scores, axis=-1, keepdims=True))
        total = jnp.sum(weights, axis=-1, keepdims=True)
        mixed = (
            jnp.dot(weights.astype(BF16), kv, preferred_element_type=F32) / total
        ).astype(BF16)
        for j in range(4):
            outs[j][rows, :] = mixed[64 * j : 64 * (j + 1), :]


def attend(packs, kvs):
    return pl.pallas_call(
        attend_kernel,
        out_shape=[jax.ShapeDtypeStruct((128, 256), BF16)] * 4,
        in_specs=[VMEM] * 8,
        out_specs=[VMEM] * 4,
        compiler_params=LIMIT,
        name="attend",
    )(*packs, *kvs)


def output_kernel(idx, acts, wo, *refs):
    mixed, out = refs[:4], refs[4]
    mine = 2 * idx[1] + idx[3]
    total = acts[...].astype(F32)
    summed = None
    for s in range(4):
        rows = pl.ds(pl.multiple_of((mine ^ s) * HV, HV), HV)
        term = jnp.dot(mixed[s][:, :HV], wo[rows, :], preferred_element_type=F32)
        summed = term if summed is None else summed + term
    attended = (total + summed).astype(BF16).astype(F32)
    out[...] = jax.nn.gelu(attended).astype(BF16)


def output(idx, acts, wo, mixed):
    return pl.pallas_call(
        output_kernel,
        out_shape=jax.ShapeDtypeStruct(acts.shape, BF16),
        in_specs=[SMEM] + [VMEM] * 6,
        out_specs=VMEM,
        compiler_params=LIMIT,
        name="output",
    )(idx, acts, wo, *mixed)


def quarter(x):
    return pl.ds(pl.multiple_of(x * 384, 384), 384)


def rows_of(p, height):
    return pl.ds(pl.multiple_of(p * height, height), height)


A_ROWS = 352


def place(ref, zz, yy, c, col, wl, ws, wp):
    for n, cc in ((0, c), (1, 1 - c)):
        p = 4 * zz + 2 * yy + cc
        base = 176 * n
        wl[rows_of(p, 96), col] = ref[base : base + 96, :]
        ws[rows_of(p, 80), col] = ref[base + 96 : base + 176, :]
        base = A_ROWS + 96 * n
        wp[rows_of(p, 96), col] = ref[base : base + 96, :]


def early_kernel(idx, skip_own, skip_oth, *refs):
    pieces, (wl, ws, wp, part, late), (skip,) = refs[:12], refs[12:17], refs[17:]
    x, y, z, c = idx[0], idx[1], idx[2], idx[3]
    last = lax.rem(z + 1, 4)
    ws[rows_of(last, 320), :] = jnp.zeros((320, 768), BF16)
    keep, got, b0, d0 = pieces[:4]
    for ref, cc in ((keep, c), (got, 1 - c)):
        p = 4 * z + 2 * y + cc
        wl[rows_of(p, 96), :] = ref[:96, :]
        ws[rows_of(p, 80), :] = ref[96:176, :]
        wp[rows_of(p, 96), :] = ref[176:, :]
    place(b0, z, 1 - y, c, quarter(x), wl, ws, wp)
    place(d0, z, 1 - y, c, quarter(1 - x), wl, ws, wp)
    for k in (1, 2):
        place_plane(pieces[4 * k : 4 * k + 4], lax.rem(z + 4 - k, 4), x, y, c, wl, ws, wp)
    for s in range(2):
        for src, cc in ((skip_own, c), (skip_oth, 1 - c)):
            skip[pl.ds(pl.multiple_of(256 * s + 128 * cc, 128), 128), :] = src[
                pl.ds(128 * s, 128), :
            ]
    for zz in range(4):

        @pl.when(last == zz)
        def _():
            late[...] = skip[:, 320 * zz : 320 * (zz + 1)]

    part[...] = jnp.dot(skip[...], ws[...], preferred_element_type=F32)


def place_plane(pieces, zz, x, y, c, wl, ws, wp):
    a, b, xa, xb = pieces
    place(a, zz, y, c, quarter(x), wl, ws, wp)
    place(b, zz, 1 - y, c, quarter(x), wl, ws, wp)
    place(xa, zz, y, c, quarter(1 - x), wl, ws, wp)
    place(xb, zz, 1 - y, c, quarter(1 - x), wl, ws, wp)


WEIGHTS = [
    jax.ShapeDtypeStruct((1536, 768), BF16),
    jax.ShapeDtypeStruct((1280, 768), BF16),
    jax.ShapeDtypeStruct((1536, 768), BF16),
]


def ordered(c, own, other):
    return jnp.where(
        c == 0, jnp.concatenate([own, other], axis=0), jnp.concatenate([other, own], axis=0)
    )


def early(idx, skip_own, skip_oth, pieces):
    return pl.pallas_call(
        early_kernel,
        out_shape=WEIGHTS
        + [jax.ShapeDtypeStruct((512, 768), F32), jax.ShapeDtypeStruct((512, 320), BF16)],
        in_specs=[SMEM] + [VMEM] * (2 + len(pieces)),
        out_specs=[VMEM] * 5,
        scratch_shapes=[pltpu.VMEM((512, 1280), BF16)],
        compiler_params=LIMIT,
        name="early",
    )(idx, skip_own, skip_oth, *pieces)


def decode_kernel(idx, depth, act_own, act_oth, far, far_oth, wl_in, ws_in, wp_in, part, late, *refs):
    del wl_in, ws_in, wp_in
    pieces, (oth, rest, wl, ws, wp), (act, spread) = refs[:4], refs[4:9], refs[9:]
    x, y, z, c = idx[0], idx[1], idx[2], idx[3]
    last = lax.rem(z + 1, 4)
    place_plane(pieces, last, x, y, c, wl, ws, wp)
    for s in range(2):
        for src, cc in ((act_own, c), (act_oth, 1 - c)):
            act[pl.ds(pl.multiple_of(128 * s + 64 * cc, 64), 64), :] = src[
                pl.ds(64 * s, 64), :
            ]
    beyond = ordered(c, far[...], far_oth[...])
    act[256:288, :] = beyond[:, :1536]
    twice = (
        lax.broadcasted_iota(jnp.int32, (256, 128), 0) // 2
        == lax.broadcasted_iota(jnp.int32, (256, 128), 1)
    ).astype(BF16)
    lifted = jnp.dot(act[...], wl[...], preferred_element_type=F32).astype(BF16)
    terms = part[...] + jnp.dot(
        late[...], ws[rows_of(last, 320), :], preferred_element_type=F32
    )
    ends = lifted[256:].astype(F32) + jnp.dot(
        beyond[:, 1536:], ws[...], preferred_element_type=F32
    )
    ends = ends.astype(BF16).astype(F32)
    taps = depth[:, pl.ds(pl.multiple_of(c * 768, 768), 768)]
    row = lax.broadcasted_iota(jnp.int32, (256, 768), 0)
    for s in range(2):
        raised = jnp.dot(twice, lifted[128 * s : 128 * (s + 1)], preferred_element_type=F32)
        here = (raised + terms[256 * s : 256 * (s + 1)]).astype(BF16).astype(F32)
        up = jnp.where(row == 0, ends[s : s + 1, :], pltpu.roll(here, 1, 0))
        down = jnp.where(row == 255, ends[s + 16 : s + 17, :], pltpu.roll(here, 255, 0))
        spread[pl.ds(256 * s, 256), :] = (
            taps[0:1] * up + taps[1:2] * here + taps[2:3] * down
        ).astype(BF16)
    for s in range(2):
        rest[pl.ds(128 * s, 128), :] = spread[
            pl.ds(pl.multiple_of(256 * s + 128 * c, 128), 128), :
        ]
    rows = jnp.concatenate(
        [
            spread[pl.ds(pl.multiple_of(256 * s + 128 * (1 - c), 128), 128), :]
            for s in range(2)
        ],
        axis=0,
    )
    oth[...] = across(rows, wp[...]).astype(BF16).reshape(oth.shape)


def decode(idx, depth, act_own, act_oth, far, far_oth, weights, part, late, pieces):
    return pl.pallas_call(
        decode_kernel,
        out_shape=[
            jax.ShapeDtypeStruct((2, 128, 1536), BF16),
            jax.ShapeDtypeStruct((256, 768), BF16),
        ]
        + WEIGHTS,
        in_specs=[SMEM] + [VMEM] * (10 + len(pieces)),
        out_specs=[VMEM] * 5,
        scratch_shapes=[pltpu.VMEM((288, 1536), BF16), pltpu.VMEM((512, 768), BF16)],
        input_output_aliases={6: 2, 7: 3, 8: 4},
        compiler_params=LIMIT,
        name="decode",
    )(idx, depth, act_own, act_oth, far, far_oth, *weights, part, late, *pieces)


def across(rows, w):
    return lax.dot_general(rows, w, (((1,), (1,)), ((), ())), preferred_element_type=F32)


def rest_kernel(rest, wp, own):
    own[...] = across(rest[...], wp[...]).reshape(own.shape)


def point_rest(rest, wp):
    return pl.pallas_call(
        rest_kernel,
        out_shape=jax.ShapeDtypeStruct((2, 128, 1536), F32),
        in_specs=[VMEM] * 2,
        out_specs=VMEM,
        compiler_params=LIMIT,
        name="point_rest",
    )(rest, wp)


def behind(v, *tokens):
    return lax.optimization_barrier((v,) + tokens)[0]


class Plan:
    def __init__(self, width, makers):
        self.width, self.makers, self.made, self.done = width, makers, {}, []

    def __getitem__(self, name):
        if name not in self.made:
            self.made[name] = self.makers[name]()
        return self.made[name]

    def send(self, how, name, free):
        v = self[name]
        if not free and len(self.done) >= self.width:
            late = self.done[: len(self.done) - self.width + 1]
            v = behind(v, *(late if CUMULATIVE else late[-1:]))
        got = how(v)
        if not free and how is not c_swap:
            self.done.append(got)
        return got


def in_hbm(v):
    return pltpu.with_memory_space_constraint(v, pltpu.HBM)


def split_kernel(idx, wl, ws, wp, keep, send, whole, sems):
    c = idx[3]
    copies = [
        pltpu.make_async_copy(src, whole.at[lo:hi], sems.at[n])
        for n, (src, lo, hi) in enumerate(((wl, 0, 96), (ws, 96, 176), (wp, 176, 272)))
    ]
    for copy in copies:
        copy.start()
    for copy, (lo, hi) in zip(copies, ((0, 96), (96, 176), (176, 272))):
        copy.wait()
        for out, cc in ((send, 1 - c), (keep, c)):
            out[lo:hi, :] = whole[lo:hi, pl.ds(pl.multiple_of(768 * cc, 768), 768)]


def split(idx, wl, ws, wp):
    return pl.pallas_call(
        split_kernel,
        out_shape=[jax.ShapeDtypeStruct((272, 768), BF16)] * 2,
        in_specs=[SMEM] + [HBM] * 3,
        out_specs=[VMEM] * 2,
        scratch_shapes=[
            pltpu.VMEM((272, 1536), BF16),
            pltpu.SemaphoreType.DMA((3,)),
        ],
        compiler_params=LIMIT,
        name="split",
    )(idx, wl, ws, wp)


def take_kernel(idx, keep, got, out, *, other):
    x = idx[0]
    cols = quarter(1 - x if other else x)
    for n, ref in enumerate((keep, got)):
        out[176 * n : 176 * (n + 1), :] = ref[:176, cols]
        out[A_ROWS + 96 * n : A_ROWS + 96 * (n + 1), :] = ref[176:, cols]


def take(idx, keep, got, other):
    return pl.pallas_call(
        functools.partial(take_kernel, other=other),
        out_shape=jax.ShapeDtypeStruct((544, 384), BF16),
        in_specs=[SMEM] + [VMEM] * 2,
        out_specs=VMEM,
        compiler_params=LIMIT,
        name="take",
    )(idx, keep, got)


def give_kernel(idx, act, skip, out):
    c = idx[3]
    out[2:16, :] = jnp.zeros((14, 2816), BF16)
    for s in range(2):
        for src, height, cols in ((act, 64, slice(0, 1536)), (skip, 128, slice(1536, 2816))):
            low, high = height * s, height * (s + 1) - 1
            out[s : s + 1, cols] = jnp.where(
                c == 0, src[low : low + 1, :], src[high : high + 1, :]
            )


def give(idx, act, skip):
    return pl.pallas_call(
        give_kernel,
        out_shape=jax.ShapeDtypeStruct((16, 2816), BF16),
        in_specs=[SMEM, VMEM, VMEM],
        out_specs=VMEM,
        compiler_params=LIMIT,
        name="give",
    )(idx, act, skip)


def on_device(
    acts, skips, norm_gain, w_query, w_key, w_value, w_out, w_lift, w_skip, depth_kernel, w_point
):
    pos = lax.axis_index("pos")
    x, c, y, z = lax.axis_index("group"), pos % 2, pos // 2 % 2, pos // 4
    idx = jnp.stack([x, y, z, c]).astype(jnp.int32)
    flat = acts.reshape(128, 1536)
    keep, send = split(idx, *map(in_hbm, (w_lift, w_skip, w_point.T)))
    got = c_swap(send)
    u0 = take(idx, keep, got, False)

    def projected():
        return project(
            idx,
            in_hbm(behind(flat, u0)),
            norm_gain.reshape(1, -1),
            *map(in_hbm, (w_query, w_key, w_value)),
        )

    def joined():
        packs = [plan[n] for n in ("q0", "qc", "qy", "qcy")]
        return jnp.concatenate(
            [p[:, :256].reshape(2, 64, 256) for p in packs], axis=1
        ).reshape(512, 256)

    def attended():
        return attend(
            [plan[n] for n in ("q0", "qc", "qy", "qcy")],
            [plan[n] for n in ("k0", "k1", "k2", "k3")],
        )

    makers = {
        "u0": lambda: u0,
        "c0": lambda: take(idx, keep, got, True),
        "packs": projected,
        "k0": joined,
        "mixes": attended,
        "act": lambda: output(idx, flat, w_out, [plan[n] for n in ("m0", "mc", "my", "mcy")]),
        "skip": lambda: jax.nn.gelu(skips.astype(F32)).astype(BF16).reshape(256, 1280),
        "edge": lambda: give(idx, plan["act"], plan["skip"]),
    }
    for n, way in enumerate(("0", "c", "y", "cy")):
        makers["p" + way] = lambda n=n: plan["packs"][n]
        makers["o" + way] = lambda n=n: plan["mixes"][n]
    makers["q0"], makers["m0"] = makers["p0"], makers["o0"]
    swaps = {"c": c_swap, "y": y_swap, "cy": cy_swap, "x": x_swap, "z": z_ring}
    swaps["beyond"], swaps["beyond c"] = over_pos(BEYOND), over_pos(BEYOND_C)

    def sender(name, how, src):
        return lambda: plan.send(swaps[how], src, name in FREE)

    for name, how, src in SENDS:
        makers[name] = sender(name, how, src)
    plan = Plan(WIDTH, makers)
    for name, _, _ in SENDS:
        plan[name]
    pieces = [keep, got, plan["b0"], plan["d0"]] + [
        plan[kind + str(k)] for k in (1, 2) for kind in "ubcd"
    ]
    *weights, part, late = early(idx, plan["skip"], plan["skipc"], pieces)
    oth, rest, *weights = decode(
        idx, depth_kernel, *(plan[n] for n in ("act", "actc", "far", "farc")), weights, part, late,
        [plan[kind + "3"] for kind in "ubcd"],
    )
    got = c_swap(oth)
    return (point_rest(rest, weights[2]) + got.astype(F32)).astype(BF16)


def extended(cells, sides, width):
    for axis, dim in sides:
        count = lax.axis_size(axis)
        ends = count - 1
        head = lax.slice_in_dim(cells, 0, width, axis=dim)
        tail = lax.slice_in_dim(cells, cells.shape[dim] - width, cells.shape[dim], axis=dim)
        cells = jnp.concatenate(
            [
                lax.ppermute(tail, axis, [(i, (i + 1) % count) for i in range(ends)]),
                cells,
                lax.ppermute(head, axis, [((i + 1) % count, i) for i in range(ends)]),
            ],
            axis=dim,
        )
    return cells


def on_device_plain(
    acts, skips, norm_gain, w_query, w_key, w_value, w_out, w_lift, w_skip, depth_kernel, w_point
):
    lift_full, skip_full, point_full = (
        lax.all_gather(w_lift, "pos", axis=0, tiled=True),
        lax.all_gather(w_skip, "pos", axis=0, tiled=True),
        lax.all_gather(w_point, "pos", axis=1, tiled=True),
    )
    seq_count, bin_rows, width = acts.shape
    actsf = acts.astype(jnp.float32)
    centre = actsf - jnp.mean(actsf, axis=-1, keepdims=True)
    normed = (
        centre * lax.rsqrt(jnp.mean(centre * centre, axis=-1, keepdims=True) + 1e-05) * norm_gain
    ).astype(jnp.bfloat16)
    flat = normed.reshape(seq_count * bin_rows, width)
    queries = (
        (jnp.dot(flat, w_query, preferred_element_type=jnp.float32) * HK ** (-0.5))
        .astype(jnp.bfloat16)
        .reshape(seq_count, bin_rows, HEADS, HK)
    )
    keys_here = (
        jnp.dot(flat, w_key, preferred_element_type=jnp.float32)
        .astype(jnp.bfloat16)
        .reshape(seq_count, bin_rows, HEADS * HK)
    )
    values_here = (
        jnp.dot(flat, w_value, preferred_element_type=jnp.float32)
        .astype(jnp.bfloat16)
        .reshape(seq_count, bin_rows, HEADS * HV)
    )
    running = jnp.full((seq_count, HEADS, bin_rows), -1e30, jnp.float32)
    key_piece = lax.all_gather(keys_here, "pos", axis=1, tiled=True)
    value_piece = lax.all_gather(values_here, "pos", axis=1, tiled=True)
    count = key_piece.shape[1]
    keyed = key_piece.reshape(seq_count, count, HEADS, HK)
    valued = value_piece.reshape(seq_count, count, HEADS, HV)
    scores = jnp.einsum("sqhd,skhd->shqk", queries, keyed, preferred_element_type=jnp.float32)
    newest = jnp.maximum(running, jnp.max(scores, axis=-1))
    weights = jnp.exp(scores - newest[..., None])
    totals = jnp.sum(weights, axis=-1)
    summed = jnp.einsum(
        "shqk,skhv->shqv", weights.astype(jnp.bfloat16), valued, preferred_element_type=jnp.float32
    )
    running, totals, summed = (newest, totals, summed)
    mixed = (
        (summed / totals[..., None])
        .transpose(0, 2, 1, 3)
        .reshape(seq_count * bin_rows, HEADS * HV)
        .astype(jnp.bfloat16)
    )
    attended = (
        actsf.reshape(seq_count * bin_rows, width)
        + jnp.dot(mixed, w_out, preferred_element_type=jnp.float32)
    ).astype(jnp.bfloat16)
    activated = jax.nn.gelu(attended.astype(jnp.float32)).astype(jnp.bfloat16)
    lifted = jnp.dot(activated, lift_full, preferred_element_type=jnp.float32)
    lifted = lifted.astype(jnp.bfloat16).reshape(seq_count, bin_rows, width)
    raised = jnp.repeat(lifted, 2, axis=1).reshape(seq_count * 2 * bin_rows, width)
    skip_act = (
        jax.nn.gelu(skips.astype(jnp.float32))
        .astype(jnp.bfloat16)
        .reshape(seq_count * 2 * bin_rows, skips.shape[2])
    )
    skip_term = jnp.dot(skip_act, skip_full, preferred_element_type=jnp.float32)
    merged = (
        (raised.astype(jnp.float32) + skip_term)
        .astype(jnp.bfloat16)
        .reshape(seq_count, 2 * bin_rows, width)
    )
    padded = extended(merged, (("pos", 1),), 1)
    paddedf = padded.astype(jnp.float32)
    spread = (
        depth_kernel[0] * paddedf[:, :-2]
        + depth_kernel[1] * paddedf[:, 1:-1]
        + depth_kernel[2] * paddedf[:, 2:]
    ).astype(jnp.bfloat16)
    spread = spread.reshape(seq_count * 2 * bin_rows, width)
    decoded = jnp.dot(spread, point_full, preferred_element_type=jnp.float32)
    return decoded.astype(jnp.bfloat16).reshape(seq_count, 2 * bin_rows, width)


def solution(mesh):
    planned = dict(mesh.shape) == {"group": 2, "pos": POS}
    return jax.shard_map(
        on_device if planned else on_device_plain,
        mesh=mesh,
        in_specs=(
            P("group", "pos", None),
            P("group", "pos", None),
            P(),
            P(),
            P(),
            P(),
            P(),
            P("pos", None),
            P("pos", None),
            P(),
            P(None, "pos"),
        ),
        out_specs=P("group", "pos", None),
        check_vma=False,
    )
```
